512 devices in a mesh: dp: 64 (over z_lo, y, core), tensor: 8 (over z_hi, x).
Axes of the slice: x: 4, y: 4, z: 16 (z_hi: 2, z_lo: 8; z = z_hi * 8 + z_lo), core: 2. Of those that a mesh axis runs over, the one named last changes fastest.
Arguments:
- query: bfloat16 [8192, 8192], P(('dp', 'tensor')), may hold values from -100 to 100
- key: bfloat16 [8192, 1024], P(('dp', 'tensor')), may hold values from -5 to 5
- value: bfloat16 [8192, 1024], P(('dp', 'tensor')), may hold values from -6 to 6
- output_cotangent: bfloat16 [8192, 8192], P(('dp', 'tensor')), may hold values from -6 to 6
- doc_lengths: int32 [16], replicated, may hold values from 1 to 768, as said below
Outputs:
- attn_out: bfloat16 [8192, 8192], P(('dp', 'tensor'))
- query_grad: bfloat16 [8192, 8192], P(('dp', 'tensor'))
- key_grad: bfloat16 [8192, 1024], P(('dp', 'tensor'))
- value_grad: bfloat16 [8192, 1024], P(('dp', 'tensor'))
The draws below stay inside these ranges and needn't reach their ends.
Inputs may be any that keep to these rules, and one draw needn't show every extreme that they name: `doc_lengths`: the sum is 8192; the first trajectory is the longest and has exactly 768 tokens.
All inputs are finite; a program needn't handle non-finite values.
Results may differ from the reference program's by a relative error of at most 0.04.
Values may be sent and summed in bfloat16 or wider, within the bound.
A program may use at most 64 MiB of HBM per device.

```python
import math
import jax
import jax.numpy as jnp
from jax import lax

HEAD_SIZE = 128
QUERY_HEADS = 64
KEY_VALUE_HEADS = 8
DEVICE_ROWS = 128
REACH = 6
DOCS = 16
TOTAL_TOKENS = 8192
MOST = 768


def shared_rows(key):
    base_offset = jnp.clip(jax.random.normal(key, (TOTAL_TOKENS, KEY_VALUE_HEADS, HEAD_SIZE), jnp.float32), -4.5, 4.5)
    return base_offset


def draw_key(key, part):
    base_offset = shared_rows(key)
    return base_offset.reshape(TOTAL_TOKENS, KEY_VALUE_HEADS * HEAD_SIZE).astype(jnp.bfloat16)


def draw_query(key, part):
    key = jax.random.fold_in(key, 5)
    fresh = jnp.clip(jax.random.normal(key, (TOTAL_TOKENS, QUERY_HEADS * HEAD_SIZE), jnp.float32), -4.5, 4.5)
    return fresh.astype(jnp.bfloat16)


def draw_doc_lengths(key, part):
    key = jax.random.fold_in(key, 7)
    rest_total = TOTAL_TOKENS - MOST
    base_length = rest_total // (DOCS - 1)
    extra_length = rest_total - base_length * (DOCS - 1)
    spread_width = max(1, min(base_length, MOST - base_length - extra_length))
    drawn_steps = jax.random.randint(key, (DOCS - 1,), 0, spread_width, dtype=jnp.int32)
    rest_lengths = base_length + drawn_steps - jnp.roll(drawn_steps, -1)
    rest_lengths = rest_lengths.at[DOCS - 2].add(extra_length)
    return jnp.concatenate([jnp.full((1,), MOST, jnp.int32), rest_lengths.astype(jnp.int32)]).astype(jnp.int32)


def levels(rng, extent, cuts, smallest, largest):
    def one(position, parts):
        draws = jax.random.uniform(jax.random.fold_in(jax.random.fold_in(rng, 6), position), (parts,), jnp.float32, smallest / len(cuts), largest / len(cuts))
        return jnp.repeat(jnp.exp(draws), extent[position] // parts).reshape((-1,) + (1,) * (len(extent) - position - 1))

    level = one(*cuts[0])
    for cut in cuts[1:]:
        level = level * one(*cut)
    return level


def normal_values(rng, extent, deviation, limit, cuts=(), kind=jnp.bfloat16):
    values = deviation * jax.random.normal(rng, extent, jnp.float32)
    if cuts:
        values = values * levels(rng, extent, cuts, -0.22, 0.18)
    return jnp.clip(values, -limit, limit).astype(kind)


def setup_inputs(seed: int = 0) -> dict:
    keys = jax.random.split(jax.random.key(seed), 6)
    return {
        "query": draw_query(jax.random.fold_in(keys[5], 71), 0),
        "key": draw_key(jax.random.fold_in(keys[5], 71), 0),
        "value": normal_values(keys[2], (TOTAL_TOKENS, KEY_VALUE_HEADS * HEAD_SIZE), 1.0, 6.0, ((0, 512),)),
        "output_cotangent": normal_values(keys[3], (TOTAL_TOKENS, QUERY_HEADS * HEAD_SIZE), 1.0, 6.0, ((0, 512),)),
        "doc_lengths": draw_doc_lengths(jax.random.fold_in(keys[5], 71), 0),
    }


NEG_FILL = -1e+30

def reference(query, key, value, output_cotangent, doc_lengths):
    query_group_count = QUERY_HEADS // KEY_VALUE_HEADS
    score_scale = 1.0 / math.sqrt(HEAD_SIZE)
    window_length = (REACH + 1) * DEVICE_ROWS
    slack_length = REACH * DEVICE_ROWS
    padded_keys = jnp.concatenate([jnp.zeros((slack_length, KEY_VALUE_HEADS * HEAD_SIZE), key.dtype), key], axis=0)
    padded_values = jnp.concatenate([jnp.zeros((slack_length, KEY_VALUE_HEADS * HEAD_SIZE), value.dtype), value], axis=0)
    doc_ends = jnp.cumsum(doc_lengths).astype(jnp.int32)
    offsets = jnp.arange(DEVICE_ROWS, dtype=jnp.int32)
    key_offsets = jnp.arange(window_length, dtype=jnp.int32)

    def segment_of(positions):
        counted = lax.optimization_barrier(jnp.sum((positions[:, None] >= doc_ends[None, :]).astype(jnp.int32), axis=1)).astype(jnp.int32)
        return jnp.where(positions >= 0, counted, -1)

    def one_block(carry, block):
        key_grads, value_grads = carry
        first_token = (block * DEVICE_ROWS).astype(jnp.int32)
        query_rows = lax.dynamic_slice_in_dim(query, first_token, DEVICE_ROWS, 0).reshape(DEVICE_ROWS, KEY_VALUE_HEADS, query_group_count, HEAD_SIZE).astype(jnp.float32)
        output_gradients = lax.dynamic_slice_in_dim(output_cotangent, first_token, DEVICE_ROWS, 0).reshape(DEVICE_ROWS, KEY_VALUE_HEADS, query_group_count, HEAD_SIZE).astype(jnp.float32)
        window_keys = lax.dynamic_slice_in_dim(padded_keys, first_token, window_length, 0).reshape(window_length, KEY_VALUE_HEADS, HEAD_SIZE).astype(jnp.float32)
        window_values = lax.dynamic_slice_in_dim(padded_values, first_token, window_length, 0).reshape(window_length, KEY_VALUE_HEADS, HEAD_SIZE).astype(jnp.float32)
        query_pos = first_token + offsets
        key_pos = first_token - slack_length + key_offsets
        allowed = (segment_of(query_pos)[:, None] == segment_of(key_pos)[None, :]) & (key_pos[None, :] <= query_pos[:, None])
        wide = allowed[:, None, None, :]
        scores = jnp.einsum('rkgd,wkd->rkgw', query_rows, window_keys) * score_scale
        scores = jnp.where(wide, scores, NEG_FILL)
        top_score = lax.optimization_barrier(jnp.max(scores, axis=-1))
        total = lax.optimization_barrier(jnp.sum(jnp.where(wide, jnp.exp(scores - top_score[..., None]), 0.0), axis=-1))
        log_total = top_score + jnp.log(total)
        probs = jnp.where(wide, jnp.exp(scores - log_total[..., None]), 0.0)
        reduced_probabilities = lax.optimization_barrier(probs.astype(jnp.bfloat16)).astype(jnp.float32)
        outputs = jnp.einsum('rkgw,wkd->rkgd', reduced_probabilities, window_values)
        delta = lax.optimization_barrier(jnp.sum(output_gradients * outputs, axis=-1))
        prob_grad = jnp.einsum('rkgd,wkd->rkgw', output_gradients, window_values)
        score_gradient = lax.optimization_barrier((probs * (prob_grad - delta[..., None])).astype(jnp.bfloat16)).astype(jnp.float32)
        query_grad = jnp.einsum('rkgw,wkd->rkgd', score_gradient, window_keys) * score_scale
        key_portion = jnp.einsum('acoh,acoe->hce', score_gradient, query_rows).reshape(window_length, KEY_VALUE_HEADS * HEAD_SIZE)
        value_portion = jnp.einsum('acoh,acoe->hce', reduced_probabilities, output_gradients).reshape(window_length, KEY_VALUE_HEADS * HEAD_SIZE)
        key_grads = lax.dynamic_update_slice_in_dim(key_grads, lax.dynamic_slice_in_dim(key_grads, first_token, window_length, 0) + key_portion, first_token, 0)
        value_grads = lax.dynamic_update_slice_in_dim(value_grads, lax.dynamic_slice_in_dim(value_grads, first_token, window_length, 0) + value_portion, first_token, 0)
        return ((key_grads, value_grads), (outputs.reshape(DEVICE_ROWS, QUERY_HEADS * HEAD_SIZE).astype(jnp.bfloat16), query_grad.reshape(DEVICE_ROWS, QUERY_HEADS * HEAD_SIZE).astype(jnp.bfloat16)))
    start_index = (jnp.zeros((TOTAL_TOKENS + slack_length, KEY_VALUE_HEADS * HEAD_SIZE), jnp.float32), jnp.zeros((TOTAL_TOKENS + slack_length, KEY_VALUE_HEADS * HEAD_SIZE), jnp.float32))
    (key_grads, value_grads), (attn_blocks, query_blocks) = lax.scan(one_block, start_index, jnp.arange(TOTAL_TOKENS // DEVICE_ROWS, dtype=jnp.int32))
    attn_out = attn_blocks.reshape(TOTAL_TOKENS, QUERY_HEADS * HEAD_SIZE)
    query_grad = query_blocks.reshape(TOTAL_TOKENS, QUERY_HEADS * HEAD_SIZE)
    key_grad = (key_grads[slack_length:] * score_scale).astype(jnp.bfloat16)
    value_grad = value_grads[slack_length:].astype(jnp.bfloat16)
    return (attn_out, query_grad, key_grad, value_grad)
```

```python
import functools
import math

import jax
import jax.numpy as jnp
from jax import lax
from jax.experimental import pallas as pl
from jax.experimental.pallas import tpu as pltpu
from jax.sharding import PartitionSpec as P

D = 128
GROUP = 8
DOCS = 16
SCALE = 1.0 / math.sqrt(D)
LOG2E = math.log2(math.e)
NEG = -1e30
MESH = pl.DeviceIdType.MESH
BF = jnp.bfloat16
F32 = jnp.float32
WIDE = 256
NT = (((1,), (1,)), ((), ()))
NN = (((1,), (0,)), ((), ()))
NEAR = [(dx, dk) for dx in (1, 3, 2, 0) for dk in (0, 1) if (dx, dk) != (0, 0)]


def dot(a, b, dims):
    return lax.dot_general(a, b, dims, preferred_element_type=F32)


def kernel(
    chips, q_in, k_in, v_in, g_in, len_ref,
    o_out, dq_out, dk_out, dv_out,
    kvw, qp, gp, qm, gm, sc, pg, pb, db, ret_out, ret_in, tot, far_out, far_in, fin, op, qgp,
    near_s, near_r, q_s, q_r, far_s, far_r, win_s, win_r, ret_s, ret_r, back_s, back_r, fin_s, fin_r, out_s, out_r,
):
    d, t = lax.axis_index("dp"), lax.axis_index("tensor")
    c, core, half, x = d // 2, d % 2, t // 4, t % 4
    piece = core * 4 + x
    head = x * 2 + core

    def device(cc, kk, hh, xx):
        return (cc * 2 + kk, hh * 4 + xx)

    def near(dx, dk):
        return (core + dk) % 2, (x + dx) % 4

    far = device(c, core, 1 - half, x)

    def copy(src, dst, ssem, rsem, to):
        return pltpu.make_async_remote_copy(
            src_ref=src, dst_ref=dst, send_sem=ssem, recv_sem=rsem, device_id=to, device_id_type=MESH
        )

    def landed(ref, sem):
        pltpu.make_async_copy(ref, ref, sem).wait()

    barrier = pltpu.get_barrier_semaphore()

    def greet(to):
        pl.semaphore_signal(barrier, inc=1, device_id=to, device_id_type=MESH)

    greet(far)
    for step in (1, 2, 3):
        pl.when(c + step < chips)(lambda: greet(device(c + step, core, half, x)))
        pl.when(c - step >= 0)(lambda: greet(device(c - step, core, half, x)))
    for dx, dk in NEAR:
        kk, xx = near(dx, dk)
        greet(device(c, kk, half, xx))

    for step in (1, 2, 3):
        @pl.when(c - step < 0)
        def _():
            for hh in (0, 1):
                kvw[hh, step] = jnp.zeros((2, D, D), BF)

        @pl.when(c + step >= chips)
        def _():
            for hh in (0, 1):
                ret_in[hh, step - 1] = jnp.zeros((2, D, D), BF)

    row = lax.broadcasted_iota(jnp.int32, (1, D), 1)
    q_pos = (2 * c + row // 64) * D + half * 64 + row % 64
    start = jnp.zeros((1, D), jnp.int32)
    end = jnp.int32(0)
    for i in range(DOCS):
        end = end + len_ref[i]
        start = jnp.where(q_pos >= end, end, start)
    key_row = lax.broadcasted_iota(jnp.int32, (D, 1), 0)

    def allowed(hh, step):
        which = half if hh == 0 else 1 - half
        k_pos = (2 * (c - step) + key_row // 64) * D + which * 64 + key_row % 64
        ok = k_pos >= start
        if step == 0:
            ok = ok & (k_pos <= q_pos)
        return ok

    up = jnp.minimum(chips - 1 - c, 3)
    down = jnp.minimum(c, 3)
    pl.semaphore_wait(barrier, 8 + up + down)

    for dx, dk in NEAR:
        kk, xx = near(dx, dk)
        cols = pl.ds(pl.multiple_of((xx * 2 + kk) * D, D), D)
        for i, ref in enumerate((k_in, v_in)):
            copy(ref.at[:, cols], kvw.at[0, 0, i, pl.ds(pl.multiple_of(piece * 16, 16), 16)], near_s, near_r,
                 device(c, kk, half, xx)).start()
    cols = pl.ds(pl.multiple_of(head * D, D), D)
    for i, ref in enumerate((k_in, v_in)):
        pltpu.make_async_copy(ref.at[:, cols], kvw.at[0, 0, i, pl.ds(pl.multiple_of(piece * 16, 16), 16)], near_r).start()
    for i, (ref, to) in enumerate(((q_in, qp), (g_in, gp))):
        for dx, dk in NEAR:
            kk, xx = near(dx, dk)
            cols = pl.ds(pl.multiple_of((xx * 2 + kk) * GROUP * D, GROUP * D), GROUP * D)
            copy(ref.at[:, cols], to.at[piece], q_s.at[i], q_r.at[i], device(c, kk, half, xx)).start()
        cols = pl.ds(pl.multiple_of(head * GROUP * D, GROUP * D), GROUP * D)
        pltpu.make_async_copy(ref.at[:, cols], to.at[piece], q_r.at[i]).start()

    landed(kvw.at[0, 0], near_r)
    crossing = [
        copy(kvw.at[0, 0, i], kvw.at[1, 0, i], far_s.at[i], far_r.at[i], far) for i in (0, 1)
    ]
    for cp in crossing:
        cp.start()

    def window(hh, i, step):
        return copy(kvw.at[hh, 0, i], kvw.at[hh, step, i], win_s.at[hh, i, step - 1], win_r.at[hh, i, step - 1],
                    device(c + step, core, half, x))

    def send_window(hh, i):
        for step in (3, 2, 1):
            pl.when(c + step < chips)(window(hh, i, step).start)

    def take_window(hh, i):
        for step in (1, 2, 3):
            pl.when(c - step >= 0)(window(hh, i, step).wait_recv)

    for i in (0, 1):
        send_window(0, i)

    def gather(pieces, rows):
        for g in range(GROUP):
            rows[g * D:(g + 1) * D, :] = pieces[:, :, g * D:(g + 1) * D].reshape(D, D)

    landed(qp, q_r.at[0])
    gather(qp, qm)

    lanes = [slice(w * WIDE, (w + 1) * WIDE) for w in range(GROUP * D // WIDE)]
    top = [jnp.full((1, WIDE), NEG, F32) for _ in lanes]
    total = [jnp.zeros((1, WIDE), F32) for _ in lanes]
    groups = [(0, (0,)), (0, (1, 2, 3)), (1, (0,)), (1, (1, 2, 3))]

    def span(hh, steps):
        return slice((hh * 4 + steps[0]) * D, (hh * 4 + steps[-1] + 1) * D)

    def block(hh, steps, i):
        return kvw[hh, steps[0]:steps[-1] + 1, i].reshape(len(steps) * D, D)

    def scores(hh, steps):
        at = span(hh, steps)
        keys = block(hh, steps, 0)
        oks = [jnp.concatenate([allowed(hh, step)] * (WIDE // D), axis=1) for step in steps]
        ok = oks[0] if len(oks) == 1 else jnp.concatenate(oks, axis=0)
        for w, lane in enumerate(lanes):
            s = jnp.where(ok, dot(keys, qm[lane, :], NT) * (SCALE * LOG2E), NEG)
            sc[at, lane] = s
            new = jnp.maximum(top[w], jnp.max(s, axis=0, keepdims=True))
            total[w] = total[w] * jnp.exp2(top[w] - new) + jnp.sum(
                jnp.exp2(sc[at, lane] - new), axis=0, keepdims=True
            )
            top[w] = new

    def prob_grads(hh, steps):
        at = span(hh, steps)
        values = block(hh, steps, 1)
        for lane in lanes:
            pg[at, lane] = dot(values, gm[lane, :], NT)

    scores(*groups[0])
    landed(gp, q_r.at[1])
    gather(gp, gm)
    prob_grads(*groups[0])
    for i in (0, 1):
        take_window(0, i)
    scores(*groups[1])
    prob_grads(*groups[1])
    for i in (0, 1):
        crossing[i].wait_recv()
        send_window(1, i)
        (scores, prob_grads)[i](*groups[2])
    take_window(1, 0)
    scores(*groups[3])

    lse = [top[w] + jnp.log(total[w]) * LOG2E for w in range(len(lanes))]
    mean = [jnp.zeros((1, WIDE), F32) for _ in lanes]

    def probs(hh, steps):
        at = span(hh, steps)
        for w, lane in enumerate(lanes):
            p = jnp.exp2(sc[at, lane] - lse[w])
            sc[at, lane] = p
            pb[at, lane] = p.astype(BF)

    def means(hh, steps):
        at = span(hh, steps)
        for w, lane in enumerate(lanes):
            mean[w] = mean[w] + jnp.sum(sc[at, lane] * pg[at, lane], axis=0, keepdims=True)

    def value_part(hh, steps):
        return dot(pb[span(hh, steps), :], gm[...], NN)

    def score_grads(hh, steps):
        at = span(hh, steps)
        for w, lane in enumerate(lanes):
            db[at, lane] = (sc[at, lane] * (pg[at, lane] - mean[w])).astype(BF)

    def key_part(hh, steps):
        return dot(db[span(hh, steps), :], qm[...], NN)

    def returned(hh, i, step):
        return copy(ret_out.at[hh, step - 1, i], ret_in.at[hh, step - 1, i], ret_s.at[hh, i, step - 1],
                    ret_r.at[hh, i, step - 1], device(c - step, core, half, x))

    def send_back(hh, i, part):
        ret_out[hh, :, i] = part.astype(BF).reshape(3, D, D)
        for step in (3, 2, 1):
            pl.when(c - step >= 0)(returned(hh, i, step).start)

    probs(*groups[3])
    send_back(1, 1, value_part(*groups[3]))
    for group in groups[:3]:
        probs(*group)
        means(*group)
    send_back(0, 1, value_part(*groups[1]))
    tot[0, 1] = value_part(*groups[0])
    tot[1, 1] = value_part(*groups[2])
    take_window(1, 1)
    prob_grads(*groups[3])
    means(*groups[3])
    score_grads(*groups[3])
    send_back(1, 0, key_part(*groups[3]))
    for group in groups[:3]:
        score_grads(*group)
    send_back(0, 0, key_part(*groups[1]))
    tot[0, 0] = key_part(*groups[0])
    tot[1, 0] = key_part(*groups[2])

    def spread(which, i, weights, pieces, out, factor):
        blocks = kvw[:, :, i].reshape(8 * D, D).T
        full = dot(blocks, weights[...], NN)
        if factor != 1.0:
            full = full * factor
        for g in range(GROUP):
            pieces[:, :, g * D:(g + 1) * D] = full[:, g * D:(g + 1) * D].T.astype(BF).reshape(8, 16, D)
        cols = pl.ds(pl.multiple_of(head * GROUP * D, GROUP * D), GROUP * D)
        for dx, dk in NEAR:
            kk, xx = near(dx, dk)
            copy(pieces.at[kk * 4 + xx], out.at[:, cols], out_s.at[which], out_r.at[which],
                 device(c, kk, half, xx)).start()
        pltpu.make_async_copy(pieces.at[piece], out.at[:, cols], out_r.at[which]).start()

    spread(0, 1, pb, op, o_out, 1.0)
    spread(1, 0, db, qgp, dq_out, SCALE)

    def total_of(hh, i):
        for step in (1, 2, 3):
            pl.when(c + step < chips)(returned(hh, i, step).wait_recv)
        out = tot[hh, i]
        for step in (1, 2, 3):
            out = out + ret_in[hh, step - 1, i].astype(F32)
        return out

    back = [copy(far_out.at[i], far_in.at[i], back_s.at[i], back_r.at[i], far) for i in (0, 1)]
    for i in (1, 0):
        far_out[i] = total_of(1, i).astype(BF)
        back[i].start()
    for i in (1, 0):
        tot[0, i] = total_of(0, i)
    cols = pl.ds(pl.multiple_of(head * D, D), D)
    for i in (1, 0):
        back[i].wait_recv()
        full = tot[0, i] + far_in[i].astype(F32)
        if i == 0:
            full = full * SCALE
        fin[i] = full.astype(BF).reshape(8, 16, D)
        out = (dk_out, dv_out)[i]
        for dx, dk in NEAR:
            kk, xx = near(dx, dk)
            copy(fin.at[i, kk * 4 + xx], out.at[:, cols], fin_s.at[i], fin_r.at[i], device(c, kk, half, xx)).start()
        pltpu.make_async_copy(fin.at[i, piece], out.at[:, cols], fin_r.at[i]).start()

    landed(kvw.at[0, 0, :, pl.ds(0, 112)], near_s)
    for i, ref in enumerate((qp, gp)):
        landed(ref.at[pl.ds(0, 7)], q_s.at[i])
    for i in (0, 1):
        crossing[i].wait_send()
        for hh in (0, 1):
            for step in (1, 2, 3):
                pl.when(c + step < chips)(window(hh, i, step).wait_send)
                pl.when(c - step >= 0)(returned(hh, i, step).wait_send)
        back[i].wait_send()
    for i, ref in enumerate((op, qgp)):
        landed(ref.at[pl.ds(0, 7)], out_s.at[i])
    for i in (1, 0):
        landed(fin.at[i, pl.ds(0, 7)], fin_s.at[i])
    for i, ref in enumerate((o_out, dq_out)):
        landed(ref, out_r.at[i])
    for i, ref in enumerate((dk_out, dv_out)):
        landed(ref, fin_r.at[i])


def per_device(query, key, value, cotangent, doc_lengths):
    chips = lax.axis_size("dp") // 2
    rows = GROUP * D
    keys = 8 * D
    sem = pltpu.SemaphoreType.DMA
    any_ = pl.BlockSpec(memory_space=pl.ANY)
    return pl.pallas_call(
        functools.partial(kernel, chips),
        out_shape=[jax.ShapeDtypeStruct(a.shape, BF) for a in (query, query, key, value)],
        in_specs=[any_] * 4 + [pl.BlockSpec(memory_space=pltpu.SMEM)],
        out_specs=[any_] * 4,
        scratch_shapes=[
            pltpu.VMEM((2, 4, 2, D, D), BF),
            pltpu.VMEM((8, 16, rows), BF),
            pltpu.VMEM((8, 16, rows), BF),
            pltpu.VMEM((rows, D), BF),
            pltpu.VMEM((rows, D), BF),
            pltpu.VMEM((keys, rows), F32),
            pltpu.VMEM((keys, rows), F32),
            pltpu.VMEM((keys, rows), BF),
            pltpu.VMEM((keys, rows), BF),
            pltpu.VMEM((2, 3, 2, D, D), BF),
            pltpu.VMEM((2, 3, 2, D, D), BF),
            pltpu.VMEM((2, 2, D, D), F32),
            pltpu.VMEM((2, D, D), BF),
            pltpu.VMEM((2, D, D), BF),
            pltpu.VMEM((2, 8, 16, D), BF),
            pltpu.VMEM((8, 16, rows), BF),
            pltpu.VMEM((8, 16, rows), BF),
            sem, sem, sem((2,)), sem((2,)), sem((2,)), sem((2,)),
            sem((2, 2, 3)), sem((2, 2, 3)), sem((2, 2, 3)), sem((2, 2, 3)),
            sem((2,)), sem((2,)), sem((2,)), sem((2,)), sem((2,)), sem((2,)),
        ],
        compiler_params=pltpu.CompilerParams(
            collective_id=0, has_side_effects=True, vmem_limit_bytes=40 << 20
        ),
        name="attention",
    )(query, key, value, cotangent, doc_lengths)


def solution(mesh):
    placed = P(("dp", "tensor"), None)
    return jax.shard_map(
        per_device,
        mesh=mesh,
        in_specs=(placed,) * 4 + (P(),),
        out_specs=(placed,) * 4,
        check_vma=False,
    )
```

```python
import functools
import math

import jax
import jax.numpy as jnp
from jax import lax
from jax.experimental import pallas as pl
from jax.experimental.pallas import tpu as pltpu
from jax.sharding import PartitionSpec as P

D = 128
GROUP = 8
DOCS = 16
SCALE = 1.0 / math.sqrt(D)
LOG2E = math.log2(math.e)
NEG = -1e30
MESH = pl.DeviceIdType.MESH
BF = jnp.bfloat16
F32 = jnp.float32
WIDE = 256
NT = (((1,), (1,)), ((), ()))
NN = (((1,), (0,)), ((), ()))
NEAR = [(dx, dk) for dx in (1, 3, 2, 0) for dk in (0, 1) if (dx, dk) != (0, 0)]


def dot(a, b, dims):
    return lax.dot_general(a, b, dims, preferred_element_type=F32)


def kernel(
    chips, q_in, k_in, v_in, g_in, len_in,
    o_out, dq_out, dk_out, dv_out,
    kvw, mid, qp, gp, qm, gm, sc, pg, pb, db, ret_out, ret_in, tot, far_out, far_in, own_out, own_in, op, qgp,
    len_ref, len_s, near_s, near_r, mid_s, mid_r, q_s, q_r, far_s, far_r, win_s, win_r, ret_s, ret_r, back_s, back_r,
    own_s, own_r, out_s, out_r,
):
    d, t = lax.axis_index("dp"), lax.axis_index("tensor")
    c, core, half, x = d // 2, d % 2, t // 4, t % 4
    piece = core * 4 + x
    head = x * 2 + core

    def device(cc, kk, hh, xx):
        return (cc * 2 + kk, hh * 4 + xx)

    def near(dx, dk):
        return (core + dk) % 2, (x + dx) % 4

    def along(by, xx, kk):
        z = (half * 8 + c // 4 + by + 16) % 16
        return device(z % 8 * 4 + c % 4, kk, z // 8, xx)

    def copy(src, dst, ssem, rsem, to):
        return pltpu.make_async_remote_copy(
            src_ref=src, dst_ref=dst, send_sem=ssem, recv_sem=rsem, device_id=to, device_id_type=MESH
        )

    def landed(ref, sem):
        pltpu.make_async_copy(ref, ref, sem).wait()

    lengths = pltpu.make_async_copy(len_in, len_ref, len_s)
    lengths.start()
    barrier = pltpu.get_barrier_semaphore()

    def greet(to):
        pl.semaphore_signal(barrier, inc=1, device_id=to, device_id_type=MESH)

    for by in (4, -4):
        greet(along(by, x, core))
    for step in (1, 2, 3):
        pl.when(c - step >= 0)(lambda: greet(device(c - step, core, half, x)))
    for dx, dk in NEAR:
        kk, xx = near(dx, dk)
        greet(device(c, kk, half, xx))

    for step in (1, 2, 3):
        @pl.when(c - step < 0)
        def _():
            for hh in (0, 1):
                kvw[hh, step] = jnp.zeros((2, D, D), BF)

        @pl.when(c + step >= chips)
        def _():
            for hh in (0, 1):
                ret_in[hh, step - 1] = jnp.zeros((2, D, D), BF)

    row = lax.broadcasted_iota(jnp.int32, (1, D), 1)
    q_pos = (2 * c + row // 64) * D + half * 64 + row % 64
    start = jnp.zeros((1, D), jnp.int32)
    end = jnp.int32(0)
    lengths.wait()
    for i in range(DOCS):
        end = end + len_ref[i]
        start = jnp.where(q_pos >= end, end, start)
    key_row = lax.broadcasted_iota(jnp.int32, (D, 1), 0)

    def allowed(hh, step):
        which = half if hh == 0 else 1 - half
        k_pos = (2 * (c - step) + key_row // 64) * D + which * 64 + key_row % 64
        ok = k_pos >= start
        if step == 0:
            ok = ok & (k_pos <= q_pos)
        return ok

    pl.semaphore_wait(barrier, 9 + jnp.minimum(chips - 1 - c, 3))

    sides = [(4, 0), (-4, 1)]
    mine = pl.ds(pl.multiple_of(piece * 16, 16), 16)

    def first_leg(i, by, side):
        cols = pl.ds(side * 4 * D, 4 * D)
        return copy((k_in, v_in)[i].at[:, cols], mid.at[i, :, cols], mid_s.at[i, side], mid_r.at[i, side], along(by, x, core))

    for i in (0, 1):
        for by, side in sides:
            first_leg(i, by, side).start()

    for dx, dk in NEAR:
        kk, xx = near(dx, dk)
        cols = pl.ds(pl.multiple_of((xx * 2 + kk) * D, D), D)
        for i, ref in enumerate((k_in, v_in)):
            copy(ref.at[:, cols], kvw.at[0, 0, i, mine], near_s, near_r,
                 device(c, kk, half, xx)).start()
    cols = pl.ds(pl.multiple_of(head * D, D), D)
    for i, ref in enumerate((k_in, v_in)):
        pltpu.make_async_copy(ref.at[:, cols], kvw.at[0, 0, i, mine], near_r).start()
    for i, (ref, to) in enumerate(((q_in, qp), (g_in, gp))):
        for dx, dk in NEAR:
            kk, xx = near(dx, dk)
            cols = pl.ds(pl.multiple_of((xx * 2 + kk) * GROUP * D, GROUP * D), GROUP * D)
            copy(ref.at[:, cols], to.at[piece], q_s.at[i], q_r.at[i], device(c, kk, half, xx)).start()
        cols = pl.ds(pl.multiple_of(head * GROUP * D, GROUP * D), GROUP * D)
        pltpu.make_async_copy(ref.at[:, cols], to.at[piece], q_r.at[i]).start()

    landed(kvw.at[0, 0], near_r)
    def window(hh, i, step):
        return copy(kvw.at[hh, 0, i], kvw.at[hh, step, i], win_s.at[hh, i, step - 1], win_r.at[hh, i, step - 1],
                    device(c + step, core, half, x))

    def send_window(hh, i):
        for step in (3, 2, 1):
            pl.when(c + step < chips)(window(hh, i, step).start)

    def take_window(hh, i):
        for step in (1, 2, 3):
            pl.when(c - step >= 0)(window(hh, i, step).wait_recv)

    for i in (0, 1):
        send_window(0, i)

    for i in (0, 1):
        for by, side in sides:
            first_leg(i, by, side).wait_recv()
        for by, side in sides:
            for j in range(4 * side, 4 * side + 4):
                copy(mid.at[i, :, pl.ds(j * D, D)], kvw.at[1, 0, i, mine], far_s.at[i], far_r.at[i],
                     along(by, j // 2, j % 2)).start()

    def gather(pieces, rows):
        for g in range(GROUP):
            rows[g * D:(g + 1) * D, :] = pieces[:, :, g * D:(g + 1) * D].reshape(D, D)

    landed(qp, q_r.at[0])
    gather(qp, qm)

    lanes = [slice(w * WIDE, (w + 1) * WIDE) for w in range(GROUP * D // WIDE)]
    top = [jnp.full((1, WIDE), NEG, F32) for _ in lanes]
    total = [jnp.zeros((1, WIDE), F32) for _ in lanes]
    groups = [(0, (0,)), (0, (1, 2, 3)), (1, (0,)), (1, (1, 2, 3))]

    def span(hh, steps):
        return slice((hh * 4 + steps[0]) * D, (hh * 4 + steps[-1] + 1) * D)

    def block(hh, steps, i):
        return kvw[hh, steps[0]:steps[-1] + 1, i].reshape(len(steps) * D, D)

    def scores(hh, steps):
        at = span(hh, steps)
        keys = block(hh, steps, 0)
        oks = [jnp.concatenate([allowed(hh, step)] * (WIDE // D), axis=1) for step in steps]
        ok = oks[0] if len(oks) == 1 else jnp.concatenate(oks, axis=0)
        for w, lane in enumerate(lanes):
            s = jnp.where(ok, dot(keys, qm[lane, :], NT) * (SCALE * LOG2E), NEG)
            sc[at, lane] = s
            new = jnp.maximum(top[w], jnp.max(s, axis=0, keepdims=True))
            total[w] = total[w] * jnp.exp2(top[w] - new) + jnp.sum(
                jnp.exp2(sc[at, lane] - new), axis=0, keepdims=True
            )
            top[w] = new

    def prob_grads(hh, steps):
        at = span(hh, steps)
        values = block(hh, steps, 1)
        for lane in lanes:
            pg[at, lane] = dot(values, gm[lane, :], NT)

    scores(*groups[0])
    landed(gp, q_r.at[1])
    gather(gp, gm)
    prob_grads(*groups[0])
    for i in (0, 1):
        take_window(0, i)
    scores(*groups[1])
    prob_grads(*groups[1])
    for i in (0, 1):
        landed(kvw.at[1, 0, i], far_r.at[i])
        send_window(1, i)
        (scores, prob_grads)[i](*groups[2])
    take_window(1, 0)
    scores(*groups[3])

    lse = [top[w] + jnp.log(total[w]) * LOG2E for w in range(len(lanes))]
    mean = [jnp.zeros((1, WIDE), F32) for _ in lanes]

    def probs(hh, steps):
        at = span(hh, steps)
        for w, lane in enumerate(lanes):
            p = jnp.exp2(sc[at, lane] - lse[w])
            sc[at, lane] = p
            pb[at, lane] = p.astype(BF)

    def means(hh, steps):
        at = span(hh, steps)
        for w, lane in enumerate(lanes):
            mean[w] = mean[w] + jnp.sum(sc[at, lane] * pg[at, lane], axis=0, keepdims=True)

    def value_part(hh, steps):
        return dot(pb[span(hh, steps), :], gm[...], NN)

    def score_grads(hh, steps):
        at = span(hh, steps)
        for w, lane in enumerate(lanes):
            db[at, lane] = (sc[at, lane] * (pg[at, lane] - mean[w])).astype(BF)

    def key_part(hh, steps):
        return dot(db[span(hh, steps), :], qm[...], NN)

    def returned(hh, i, step):
        return copy(ret_out.at[hh, step - 1, i], ret_in.at[hh, step - 1, i], ret_s.at[hh, i, step - 1],
                    ret_r.at[hh, i, step - 1], device(c - step, core, half, x))

    def send_back(hh, i, part):
        ret_out[hh, :, i] = part.astype(BF).reshape(3, D, D)
        for step in (3, 2, 1):
            pl.when(c - step >= 0)(returned(hh, i, step).start)

    def spread(which, i, weights, pieces, out, factor):
        blocks = kvw[:, :, i].reshape(8 * D, D).T
        full = dot(blocks, weights[...], NN)
        if factor != 1.0:
            full = full * factor
        for g in range(GROUP):
            pieces[:, :, g * D:(g + 1) * D] = full[:, g * D:(g + 1) * D].T.astype(BF).reshape(8, 16, D)
        cols = pl.ds(pl.multiple_of(head * GROUP * D, GROUP * D), GROUP * D)
        for dx, dk in NEAR:
            kk, xx = near(dx, dk)
            copy(pieces.at[kk * 4 + xx], out.at[:, cols], out_s.at[which], out_r.at[which],
                 device(c, kk, half, xx)).start()
        pltpu.make_async_copy(pieces.at[piece], out.at[:, cols], out_r.at[which]).start()

    def total_of(hh, i, part):
        for step in (1, 2, 3):
            pl.when(c + step < chips)(returned(hh, i, step).wait_recv)
        for step in (1, 2, 3):
            part = part + ret_in[hh, step - 1, i].astype(F32)
        return part.astype(BF)

    def cross(i):
        far_out[i] = total_of(1, i, tot[1, i])
        for p in range(8):
            copy(far_out.at[i, pl.ds(p * 16, 16)], far_in.at[i, pl.ds(pl.multiple_of(head * 16, 16), 16)],
                 back_s.at[i], back_r.at[i], along(8, p % 4, p // 4)).start()

    probs(*groups[3])
    send_back(1, 1, value_part(*groups[3]))
    for group in groups[:3]:
        probs(*group)
        means(*group)
    take_window(1, 1)
    prob_grads(*groups[3])
    means(*groups[3])
    score_grads(*groups[3])
    send_back(1, 0, key_part(*groups[3]))
    tot[1, 1] = value_part(*groups[2])
    score_grads(*groups[2])
    tot[1, 0] = key_part(*groups[2])
    send_back(0, 1, value_part(*groups[1]))
    score_grads(*groups[1])
    send_back(0, 0, key_part(*groups[1]))
    cross(1)
    spread(0, 1, pb, op, o_out, 1.0)
    cross(0)
    score_grads(*groups[0])
    spread(1, 0, db, qgp, dq_out, SCALE)
    tot[0, 1] = value_part(*groups[0])
    tot[0, 0] = key_part(*groups[0])
    to = pl.ds(pl.multiple_of(head * 16, 16), 16)
    for i in (1, 0):
        own_out[i] = total_of(0, i, tot[0, i])
        for dx, dk in NEAR:
            kk, xx = near(dx, dk)
            copy(own_out.at[i, pl.ds(pl.multiple_of((kk * 4 + xx) * 16, 16), 16)], own_in.at[i, to], own_s.at[i],
                 own_r.at[i], device(c, kk, half, xx)).start()
        pltpu.make_async_copy(own_out.at[i, mine], own_in.at[i, to], own_r.at[i]).start()
    for i, (out, factor) in ((1, (dv_out, 1.0)), (0, (dk_out, SCALE))):
        landed(own_in.at[i], own_r.at[i])
        landed(far_in.at[i], back_r.at[i])
        for j in range(8):
            both = own_in[i, j * 16:(j + 1) * 16].astype(F32) + far_in[i, j * 16:(j + 1) * 16].astype(F32)
            out[:, j * D:(j + 1) * D] = (both * factor).astype(BF)

    landed(kvw.at[0, 0, :, pl.ds(0, 112)], near_s)
    for i, ref in enumerate((qp, gp)):
        landed(ref.at[pl.ds(0, 7)], q_s.at[i])
    for i in (0, 1):
        for by, side in sides:
            first_leg(i, by, side).wait_send()
        landed(kvw.at[1, 0, i], far_s.at[i])
        for hh in (0, 1):
            for step in (1, 2, 3):
                pl.when(c + step < chips)(window(hh, i, step).wait_send)
                pl.when(c - step >= 0)(returned(hh, i, step).wait_send)
        landed(far_out.at[i], back_s.at[i])
        landed(own_out.at[i, pl.ds(0, 112)], own_s.at[i])
    for i, ref in enumerate((op, qgp)):
        landed(ref.at[pl.ds(0, 7)], out_s.at[i])
    for i, ref in enumerate((o_out, dq_out)):
        landed(ref, out_r.at[i])


def write_out(a, b, c, d, ao, bo, co, do, sems):
    copies = [pltpu.make_async_copy(src, dst, sems.at[i]) for i, (src, dst) in enumerate(((a, ao), (b, bo), (c, co), (d, do)))]
    for cp in copies:
        cp.start()
    for cp in copies:
        cp.wait()


def per_device(query, key, value, cotangent, doc_lengths):
    chips = lax.axis_size("dp") // 2
    rows = GROUP * D
    keys = 8 * D
    sem = pltpu.SemaphoreType.DMA
    any_ = pl.BlockSpec(memory_space=pl.ANY)
    vmem = pl.BlockSpec(memory_space=pltpu.VMEM)
    parts = pl.pallas_call(
        functools.partial(kernel, chips),
        out_shape=[jax.ShapeDtypeStruct(a.shape, BF) for a in (query, query, key, value)],
        in_specs=[any_] * 5,
        out_specs=[vmem] * 4,
        scratch_shapes=[
            pltpu.VMEM((2, 4, 2, D, D), BF),
            pltpu.VMEM((2, 16, 8 * D), BF),
            pltpu.VMEM((8, 16, rows), BF),
            pltpu.VMEM((8, 16, rows), BF),
            pltpu.VMEM((rows, D), BF),
            pltpu.VMEM((rows, D), BF),
            pltpu.VMEM((keys, rows), F32),
            pltpu.VMEM((keys, rows), F32),
            pltpu.VMEM((keys, rows), BF),
            pltpu.VMEM((keys, rows), BF),
            pltpu.VMEM((2, 3, 2, D, D), BF),
            pltpu.VMEM((2, 3, 2, D, D), BF),
            pltpu.VMEM((2, 2, D, D), F32),
            pltpu.VMEM((2, D, D), BF),
            pltpu.VMEM((2, D, D), BF),
            pltpu.VMEM((2, D, D), BF),
            pltpu.VMEM((2, D, D), BF),
            pltpu.VMEM((8, 16, rows), BF),
            pltpu.VMEM((8, 16, rows), BF),
            pltpu.SMEM((DOCS,), jnp.int32), sem,
            sem, sem, sem((2, 2)), sem((2, 2)), sem((2,)), sem((2,)), sem((2,)), sem((2,)),
            sem((2, 2, 3)), sem((2, 2, 3)), sem((2, 2, 3)), sem((2, 2, 3)),
            sem((2,)), sem((2,)), sem((2,)), sem((2,)), sem((2,)), sem((2,)),
        ],
        compiler_params=pltpu.CompilerParams(
            collective_id=0, has_side_effects=True, vmem_limit_bytes=60 << 20
        ),
        name="attention",
    )(query, key, value, cotangent, doc_lengths)
    return pl.pallas_call(
        write_out,
        out_shape=[jax.ShapeDtypeStruct(a.shape, BF) for a in parts],
        in_specs=[vmem] * 4,
        out_specs=[any_] * 4,
        scratch_shapes=[sem((4,))],
        name="write_out",
    )(*parts)


def solution(mesh):
    placed = P(("dp", "tensor"), None)
    return jax.shard_map(
        per_device,
        mesh=mesh,
        in_specs=(placed,) * 4 + (P(),),
        out_specs=(placed,) * 4,
        check_vma=False,
    )
```

```python
import functools
import math

import jax
import jax.numpy as jnp
from jax import lax
from jax.experimental import pallas as pl
from jax.experimental.pallas import tpu as pltpu
from jax.sharding import PartitionSpec as P

D = 128
GROUP = 8
DOCS = 16
SCALE = 1.0 / math.sqrt(D)
LOG2E = math.log2(math.e)
NEG = -1e30
RING = 4
MESH = pl.DeviceIdType.MESH
BF = jnp.bfloat16
F32 = jnp.float32
WIDE = 256
NT = (((1,), (1,)), ((), ()))
NN = (((1,), (0,)), ((), ()))
NEAR = [(dx, dk) for dx in (1, 3, 2, 0) for dk in (0, 1) if (dx, dk) != (0, 0)]


def dot(a, b, dims):
    return lax.dot_general(a, b, dims, preferred_element_type=F32)


def kernel(
    chips, q_in, k_in, v_in, g_in, len_in,
    o_out, dq_out, dk_out, dv_out,
    kvw, mid, qp, gp, qm, gm, sc, pg, pb, db, ret_out, ret_in, tot, far_out, far_in, own_out, own_in, op, qgp,
    way, part_in, part_sum, plane_in,
    len_ref, len_s, ring_met, plane_met, near_s, near_r, mid_s, mid_r, q_s, q_r, far_s, far_r, win_s, win_r, ret_s, ret_r, back_s, back_r,
    own_s, own_r, out_s, out_r, way_s, way_r, part_s, part_r, plane_s, plane_r,
):
    d, t = lax.axis_index("dp"), lax.axis_index("tensor")
    c, core, half, x = d // 2, d % 2, t // 4, t % 4
    z_lo, y = c // RING, c % RING
    piece = core * 4 + x
    head = x * 2 + core

    def device(cc, kk, hh, xx):
        return (cc * 2 + kk, hh * 4 + xx)

    def near(dx, dk):
        return (core + dk) % 2, (x + dx) % 4

    def along(by, xx, kk):
        z = (half * 8 + z_lo + by + 16) % 16
        return device(z % 8 * RING + y, kk, z // 8, xx)

    def copy(src, dst, ssem, rsem, to):
        return pltpu.make_async_remote_copy(
            src_ref=src, dst_ref=dst, send_sem=ssem, recv_sem=rsem, device_id=to, device_id_type=MESH
        )

    def landed(ref, sem):
        pltpu.make_async_copy(ref, ref, sem).wait()

    lengths = pltpu.make_async_copy(len_in, len_ref, len_s)
    lengths.start()
    barrier = pltpu.get_barrier_semaphore()

    def greet(to):
        pl.semaphore_signal(barrier, inc=1, device_id=to, device_id_type=MESH)

    def across(by):
        return device(z_lo * RING + (y + by) % RING, core, half, x)

    for by in (4, -4, 1, -1):
        greet(along(by, x, core))
    for by in (1, 3):
        greet(across(by))
    for dx, dk in NEAR:
        kk, xx = near(dx, dk)
        greet(device(c, kk, half, xx))

    for step in (1, 2, 3):
        @pl.when(c - step < 0)
        def _():
            for hh in (0, 1):
                kvw[hh, step] = jnp.zeros((2, D, D), BF)

        @pl.when(c + step >= chips)
        def _():
            ret_in[1, step - 1] = jnp.zeros((2, D, D), BF)

        @pl.when(y + step >= RING)
        def _():
            ret_in[0, step - 1] = jnp.zeros((2, D, D), BF)

        @pl.when(y - step < 0)
        def _():
            part_in[step - 1] = jnp.zeros((2, D, D), BF)

    takes = (z_lo > 0) & (y > 0)
    gives = (c + RING < chips) & (y > 0)

    @pl.when(jnp.logical_not(gives))
    def _():
        plane_in[...] = jnp.zeros((2, D, D), BF)

    row = lax.broadcasted_iota(jnp.int32, (1, D), 1)
    q_pos = (2 * c + row // 64) * D + half * 64 + row % 64
    start = jnp.zeros((1, D), jnp.int32)
    end = jnp.int32(0)
    lengths.wait()
    for i in range(DOCS):
        end = end + len_ref[i]
        start = jnp.where(q_pos >= end, end, start)
    key_row = lax.broadcasted_iota(jnp.int32, (D, 1), 0)

    def allowed(hh, step):
        which = half if hh == 0 else 1 - half
        k_pos = (2 * (c - step) + key_row // 64) * D + which * 64 + key_row % 64
        ok = k_pos >= start
        if step == 0:
            ok = ok & (k_pos <= q_pos)
        return ok

    pl.semaphore_wait(barrier, 13)

    for by in (1, 3):
        pl.semaphore_signal(ring_met, inc=1, device_id=across(by), device_id_type=MESH)

    sides = [(4, 0), (-4, 1)]
    mine = pl.ds(pl.multiple_of(piece * 16, 16), 16)

    def first_leg(i, by, side):
        cols = pl.ds(side * 4 * D, 4 * D)
        return copy((k_in, v_in)[i].at[:, cols], mid.at[i, :, cols], mid_s.at[i, side], mid_r.at[i, side], along(by, x, core))

    for i in (0, 1):
        for by, side in sides:
            first_leg(i, by, side).start()

    for dx, dk in NEAR:
        kk, xx = near(dx, dk)
        cols = pl.ds(pl.multiple_of((xx * 2 + kk) * D, D), D)
        for i, ref in enumerate((k_in, v_in)):
            copy(ref.at[:, cols], kvw.at[0, 0, i, mine], near_s, near_r,
                 device(c, kk, half, xx)).start()
    cols = pl.ds(pl.multiple_of(head * D, D), D)
    for i, ref in enumerate((k_in, v_in)):
        pltpu.make_async_copy(ref.at[:, cols], kvw.at[0, 0, i, mine], near_r).start()
    pl.semaphore_wait(ring_met, 2)
    pl.semaphore_signal(plane_met, inc=1, device_id=along(-1, x, core), device_id_type=MESH)
    for i, (ref, to) in enumerate(((q_in, qp), (g_in, gp))):
        for dx, dk in NEAR:
            kk, xx = near(dx, dk)
            cols = pl.ds(pl.multiple_of((xx * 2 + kk) * GROUP * D, GROUP * D), GROUP * D)
            copy(ref.at[:, cols], to.at[piece], q_s.at[i], q_r.at[i], device(c, kk, half, xx)).start()
        cols = pl.ds(pl.multiple_of(head * GROUP * D, GROUP * D), GROUP * D)
        pltpu.make_async_copy(ref.at[:, cols], to.at[piece], q_r.at[i]).start()

    pl.semaphore_wait(plane_met, 1)
    landed(kvw.at[0, 0], near_r)
    def window(hh, i, step):
        return copy(kvw.at[hh, 0, i], kvw.at[hh, step, i], win_s.at[hh, i, step - 1], win_r.at[hh, i, step - 1],
                    device(c + step, core, half, x))

    def to_next_plane(i):
        return copy(kvw.at[0, 0, i], way.at[i], way_s.at[i], way_r.at[i], device(c + RING, core, half, x))

    def round_plane(i, back):
        return copy(way.at[i], kvw.at[0, RING - back, i], win_s.at[0, i, 3 - back], win_r.at[0, i, 3 - back],
                    device(c - back, core, half, x))

    def send_window(hh, i):
        if hh == 0:
            pl.when(gives)(to_next_plane(i).start)
        for step in (3, 2, 1):
            pl.when(y + step < RING if hh == 0 else c + step < chips)(window(hh, i, step).start)

    def take_window(hh, i):
        for step in (1, 2, 3):
            pl.when(c - step >= 0)(window(hh, i, step).wait_recv)

    for i in (0, 1):
        send_window(0, i)

    for i in (0, 1):
        for by, side in sides:
            first_leg(i, by, side).wait_recv()
        for by, side in sides:
            for j in range(4 * side, 4 * side + 4):
                copy(mid.at[i, :, pl.ds(j * D, D)], kvw.at[1, 0, i, mine], far_s.at[i], far_r.at[i],
                     along(by, j // 2, j % 2)).start()

    def gather(pieces, rows):
        for g in range(GROUP):
            rows[g * D:(g + 1) * D, :] = pieces[:, :, g * D:(g + 1) * D].reshape(D, D)

    for i in (0, 1):
        pl.when(takes)(to_next_plane(i).wait_recv)
        for back in (1, 2, 3):
            pl.when(takes & (y - back >= 0))(round_plane(i, back).start)

    for i in (0, 1):
        landed(kvw.at[1, 0, i], far_r.at[i])
        send_window(1, i)

    landed(qp, q_r.at[0])
    gather(qp, qm)

    lanes = [slice(w * WIDE, (w + 1) * WIDE) for w in range(GROUP * D // WIDE)]
    top = [jnp.full((1, WIDE), NEG, F32) for _ in lanes]
    total = [jnp.zeros((1, WIDE), F32) for _ in lanes]
    groups = [(0, (0,)), (0, (1, 2, 3)), (1, (0,)), (1, (1, 2, 3))]

    def span(hh, steps):
        return slice((hh * 4 + steps[0]) * D, (hh * 4 + steps[-1] + 1) * D)

    def block(hh, steps, i):
        return kvw[hh, steps[0]:steps[-1] + 1, i].reshape(len(steps) * D, D)

    def scores(hh, steps):
        at = span(hh, steps)
        keys = block(hh, steps, 0)
        oks = [jnp.concatenate([allowed(hh, step)] * (WIDE // D), axis=1) for step in steps]
        ok = oks[0] if len(oks) == 1 else jnp.concatenate(oks, axis=0)
        for w, lane in enumerate(lanes):
            s = jnp.where(ok, dot(keys, qm[lane, :], NT) * (SCALE * LOG2E), NEG)
            sc[at, lane] = s
            new = jnp.maximum(top[w], jnp.max(s, axis=0, keepdims=True))
            total[w] = total[w] * jnp.exp2(top[w] - new) + jnp.sum(
                jnp.exp2(sc[at, lane] - new), axis=0, keepdims=True
            )
            top[w] = new

    def prob_grads(hh, steps):
        at = span(hh, steps)
        values = block(hh, steps, 1)
        for lane in lanes:
            pg[at, lane] = dot(values, gm[lane, :], NT)

    landed(gp, q_r.at[1])
    gather(gp, gm)
    for group in (groups[0], groups[2]):
        scores(*group)
        prob_grads(*group)
    for i in (0, 1):
        take_window(0, i)
    scores(*groups[1])
    prob_grads(*groups[1])
    take_window(1, 0)
    scores(*groups[3])

    lse = [top[w] + jnp.log(total[w]) * LOG2E for w in range(len(lanes))]
    mean = [jnp.zeros((1, WIDE), F32) for _ in lanes]

    def probs(hh, steps):
        at = span(hh, steps)
        for w, lane in enumerate(lanes):
            p = jnp.exp2(sc[at, lane] - lse[w])
            sc[at, lane] = p
            pb[at, lane] = p.astype(BF)

    def means(hh, steps):
        at = span(hh, steps)
        for w, lane in enumerate(lanes):
            mean[w] = mean[w] + jnp.sum(sc[at, lane] * pg[at, lane], axis=0, keepdims=True)

    def value_part(hh, steps):
        return dot(pb[span(hh, steps), :], gm[...], NN)

    def score_grads(hh, steps):
        at = span(hh, steps)
        for w, lane in enumerate(lanes):
            db[at, lane] = (sc[at, lane] * (pg[at, lane] - mean[w])).astype(BF)

    def key_part(hh, steps):
        return dot(db[span(hh, steps), :], qm[...], NN)

    def returned(hh, i, step):
        return copy(ret_out.at[hh, step - 1, i], ret_in.at[hh, step - 1, i], ret_s.at[hh, i, step - 1],
                    ret_r.at[hh, i, step - 1], device(c - step, core, half, x))

    def in_plane(i, ahead):
        return copy(ret_out.at[0, 3 - ahead, i], part_in.at[ahead - 1, i], part_s.at[i, ahead - 1],
                    part_r.at[i, ahead - 1], device(c + ahead, core, half, x))

    def to_last_plane(i):
        return copy(part_sum.at[i], plane_in.at[i], plane_s.at[i], plane_r.at[i], device(c - RING, core, half, x))

    def send_back(hh, i, part):
        ret_out[hh, :, i] = part.astype(BF).reshape(3, D, D)
        for step in (3, 2, 1):
            if hh == 0:
                ahead = RING - step
                pl.when((z_lo > 0) & (y + ahead < RING))(in_plane(i, ahead).start)
                pl.when(y - step >= 0)(returned(hh, i, step).start)
            else:
                pl.when(c - step >= 0)(returned(hh, i, step).start)

    def pass_back(i):
        for ahead in (1, 2, 3):
            pl.when(takes & (y - ahead >= 0))(in_plane(i, ahead).wait_recv)

        @pl.when(takes)
        def _():
            part = part_in[0, i].astype(F32)
            for ahead in (2, 3):
                part = part + part_in[ahead - 1, i].astype(F32)
            part_sum[i] = part.astype(BF)
            to_last_plane(i).start()

    def spread(which, i, weights, pieces, out, factor):
        blocks = kvw[:, :, i].reshape(8 * D, D).T
        full = dot(blocks, weights[...], NN)
        if factor != 1.0:
            full = full * factor
        for g in range(GROUP):
            pieces[:, :, g * D:(g + 1) * D] = full[:, g * D:(g + 1) * D].T.astype(BF).reshape(8, 16, D)
        cols = pl.ds(pl.multiple_of(head * GROUP * D, GROUP * D), GROUP * D)
        for dx, dk in NEAR:
            kk, xx = near(dx, dk)
            copy(pieces.at[kk * 4 + xx], out.at[:, cols], out_s.at[which], out_r.at[which],
                 device(c, kk, half, xx)).start()
        pltpu.make_async_copy(pieces.at[piece], out.at[:, cols], out_r.at[which]).start()

    def total_of(hh, i, part):
        for step in (1, 2, 3):
            pl.when(y + step < RING if hh == 0 else c + step < chips)(returned(hh, i, step).wait_recv)
        if hh == 0:
            pl.when(gives)(to_last_plane(i).wait_recv)
            part = part + plane_in[i].astype(F32)
        for step in (1, 2, 3):
            part = part + ret_in[hh, step - 1, i].astype(F32)
        return part.astype(BF)

    def cross(i):
        far_out[i] = total_of(1, i, tot[1, i])
        for p in range(8):
            copy(far_out.at[i, pl.ds(p * 16, 16)], far_in.at[i, pl.ds(pl.multiple_of(head * 16, 16), 16)],
                 back_s.at[i], back_r.at[i], along(8, p % 4, p // 4)).start()

    probs(*groups[3])
    send_back(1, 1, value_part(*groups[3]))
    for group in groups[:3]:
        probs(*group)
        means(*group)
    take_window(1, 1)
    prob_grads(*groups[3])
    means(*groups[3])
    score_grads(*groups[3])
    send_back(1, 0, key_part(*groups[3]))
    tot[1, 1] = value_part(*groups[2])
    score_grads(*groups[2])
    tot[1, 0] = key_part(*groups[2])
    send_back(0, 1, value_part(*groups[1]))
    score_grads(*groups[1])
    send_back(0, 0, key_part(*groups[1]))
    cross(1)
    pass_back(1)
    spread(0, 1, pb, op, o_out, 1.0)
    cross(0)
    pass_back(0)
    score_grads(*groups[0])
    spread(1, 0, db, qgp, dq_out, SCALE)
    tot[0, 1] = value_part(*groups[0])
    tot[0, 0] = key_part(*groups[0])
    to = pl.ds(pl.multiple_of(head * 16, 16), 16)
    for i in (1, 0):
        own_out[i] = total_of(0, i, tot[0, i])
        for dx, dk in NEAR:
            kk, xx = near(dx, dk)
            copy(own_out.at[i, pl.ds(pl.multiple_of((kk * 4 + xx) * 16, 16), 16)], own_in.at[i, to], own_s.at[i],
                 own_r.at[i], device(c, kk, half, xx)).start()
        pltpu.make_async_copy(own_out.at[i, mine], own_in.at[i, to], own_r.at[i]).start()
    for i, (out, factor) in ((1, (dv_out, 1.0)), (0, (dk_out, SCALE))):
        landed(own_in.at[i], own_r.at[i])
        landed(far_in.at[i], back_r.at[i])
        for j in range(8):
            both = own_in[i, j * 16:(j + 1) * 16].astype(F32) + far_in[i, j * 16:(j + 1) * 16].astype(F32)
            out[:, j * D:(j + 1) * D] = (both * factor).astype(BF)

    landed(kvw.at[0, 0, :, pl.ds(0, 112)], near_s)
    for i, ref in enumerate((qp, gp)):
        landed(ref.at[pl.ds(0, 7)], q_s.at[i])
    for i in (0, 1):
        for by, side in sides:
            first_leg(i, by, side).wait_send()
        landed(kvw.at[1, 0, i], far_s.at[i])
        pl.when(gives)(to_next_plane(i).wait_send)
        pl.when(takes)(to_last_plane(i).wait_send)
        for step in (1, 2, 3):
            pl.when(y + step < RING)(window(0, i, step).wait_send)
            pl.when(takes & (y - step >= 0))(round_plane(i, step).wait_send)
            pl.when(c + step < chips)(window(1, i, step).wait_send)
            pl.when((z_lo > 0) & (y + step < RING))(in_plane(i, step).wait_send)
            pl.when(y - step >= 0)(returned(0, i, step).wait_send)
            pl.when(c - step >= 0)(returned(1, i, step).wait_send)
        landed(far_out.at[i], back_s.at[i])
        landed(own_out.at[i, pl.ds(0, 112)], own_s.at[i])
    for i, ref in enumerate((op, qgp)):
        landed(ref.at[pl.ds(0, 7)], out_s.at[i])
    for i, ref in enumerate((o_out, dq_out)):
        landed(ref, out_r.at[i])


def write_out(a, b, c, d, ao, bo, co, do, sems):
    copies = [
        pltpu.make_async_copy(src, dst, sems.at[i]) for i, (src, dst) in enumerate(((a, ao), (b, bo), (c, co), (d, do)))
    ]
    for cp in copies:
        cp.start()
    for cp in copies:
        cp.wait()


def per_device(query, key, value, cotangent, doc_lengths):
    chips = lax.axis_size("dp") // 2
    rows = GROUP * D
    keys = 8 * D
    sem = pltpu.SemaphoreType.DMA
    any_ = pl.BlockSpec(memory_space=pl.ANY)
    vmem = pl.BlockSpec(memory_space=pltpu.VMEM)
    parts = pl.pallas_call(
        functools.partial(kernel, chips),
        out_shape=[jax.ShapeDtypeStruct(a.shape, BF) for a in (query, query, key, value)],
        in_specs=[any_] * 5,
        out_specs=[vmem] * 4,
        scratch_shapes=[
            pltpu.VMEM((2, 4, 2, D, D), BF),
            pltpu.VMEM((2, 16, 8 * D), BF),
            pltpu.VMEM((8, 16, rows), BF),
            pltpu.VMEM((8, 16, rows), BF),
            pltpu.VMEM((rows, D), BF),
            pltpu.VMEM((rows, D), BF),
            pltpu.VMEM((keys, rows), F32),
            pltpu.VMEM((keys, rows), F32),
            pltpu.VMEM((keys, rows), BF),
            pltpu.VMEM((keys, rows), BF),
            pltpu.VMEM((2, 3, 2, D, D), BF),
            pltpu.VMEM((2, 3, 2, D, D), BF),
            pltpu.VMEM((2, 2, D, D), F32),
            pltpu.VMEM((2, D, D), BF),
            pltpu.VMEM((2, D, D), BF),
            pltpu.VMEM((2, D, D), BF),
            pltpu.VMEM((2, D, D), BF),
            pltpu.VMEM((8, 16, rows), BF),
            pltpu.VMEM((8, 16, rows), BF),
            pltpu.VMEM((2, D, D), BF),
            pltpu.VMEM((3, 2, D, D), BF),
            pltpu.VMEM((2, D, D), BF),
            pltpu.VMEM((2, D, D), BF),
            pltpu.SMEM((DOCS,), jnp.int32), sem, pltpu.SemaphoreType.REGULAR, pltpu.SemaphoreType.REGULAR,
            sem, sem, sem((2, 2)), sem((2, 2)), sem((2,)), sem((2,)), sem((2,)), sem((2,)),
            sem((2, 2, 3)), sem((2, 2, 3)), sem((2, 2, 3)), sem((2, 2, 3)),
            sem((2,)), sem((2,)), sem((2,)), sem((2,)), sem((2,)), sem((2,)),
            sem((2,)), sem((2,)), sem((2, 3)), sem((2, 3)), sem((2,)), sem((2,)),
        ],
        compiler_params=pltpu.CompilerParams(
            collective_id=0, has_side_effects=True, vmem_limit_bytes=60 << 20
        ),
        name="attention",
    )(query, key, value, cotangent, doc_lengths)
    return pl.pallas_call(
        write_out,
        out_shape=[jax.ShapeDtypeStruct(a.shape, BF) for a in parts],
        in_specs=[vmem] * 4,
        out_specs=[any_] * 4,
        scratch_shapes=[sem((4,))],
        name="write_out",
    )(*parts)


def solution(mesh):
    placed = P(("dp", "tensor"), None)
    return jax.shard_map(
        per_device,
        mesh=mesh,
        in_specs=(placed,) * 4 + (P(),),
        out_specs=(placed,) * 4,
        check_vma=False,
    )
```

```python
import functools
import math

import jax
import jax.numpy as jnp
from jax import lax
from jax.experimental import pallas as pl
from jax.experimental.pallas import tpu as pltpu
from jax.sharding import PartitionSpec as P

D = 128
GROUP = 8
DOCS = 16
SCALE = 1.0 / math.sqrt(D)
LOG2E = math.log2(math.e)
NEG = -1e30
RING = 4
MESH = pl.DeviceIdType.MESH
BF = jnp.bfloat16
F32 = jnp.float32
WIDE = 256
NT = (((1,), (1,)), ((), ()))
NN = (((1,), (0,)), ((), ()))
NEAR = [(dx, dk) for dx in (1, 3, 2, 0) for dk in (0, 1) if (dx, dk) != (0, 0)]


def dot(a, b, dims):
    return lax.dot_general(a, b, dims, preferred_element_type=F32)


def kernel(
    chips, q_in, k_in, v_in, g_in, len_in,
    o_out, dq_out, dk_out, dv_out,
    kvw, mid, qp, gp, qm, gm, sc, pg, pb, db, ret_out, ret_in, tot, far_out, far_in, own_out, own_in, op, qgp,
    way, part_in, part_sum, plane_in, raw, raw_s,
    len_ref, len_s, ring_met, plane_met, near_s, near_r, mid_s, mid_r, q_s, q_r, far_s, far_r, win_s, win_r, ret_s, ret_r, back_s, back_r,
    own_s, own_r, out_s, out_r, way_s, way_r, part_s, part_r, plane_s, plane_r,
):
    d, t = lax.axis_index("dp"), lax.axis_index("tensor")
    c, core, half, x = d // 2, d % 2, t // 4, t % 4
    z_lo, y = c // RING, c % RING
    piece = core * 4 + x
    head = x * 2 + core

    def device(cc, kk, hh, xx):
        return (cc * 2 + kk, hh * 4 + xx)

    def near(dx, dk):
        return (core + dk) % 2, (x + dx) % 4

    def along(by, xx, kk):
        z = (half * 8 + z_lo + by + 16) % 16
        return device(z % 8 * RING + y, kk, z // 8, xx)

    def copy(src, dst, ssem, rsem, to):
        return pltpu.make_async_remote_copy(
            src_ref=src, dst_ref=dst, send_sem=ssem, recv_sem=rsem, device_id=to, device_id_type=MESH
        )

    def landed(ref, sem):
        pltpu.make_async_copy(ref, ref, sem).wait()

    lengths = pltpu.make_async_copy(len_in, len_ref, len_s)
    lengths.start()
    here = [pltpu.make_async_copy((k_in, v_in)[i], raw.at[i], raw_s.at[i]) for i in (0, 1)]
    for cp in here:
        cp.start()
    barrier = pltpu.get_barrier_semaphore()

    def greet(to):
        pl.semaphore_signal(barrier, inc=1, device_id=to, device_id_type=MESH)

    def across(by):
        return device(z_lo * RING + (y + by) % RING, core, half, x)

    for by in (4, -4, 1, -1):
        greet(along(by, x, core))
    for by in (1, 3):
        greet(across(by))
    for dx, dk in NEAR:
        kk, xx = near(dx, dk)
        greet(device(c, kk, half, xx))

    for step in (1, 2, 3):
        @pl.when(c - step < 0)
        def _():
            for hh in (0, 1):
                kvw[hh, step] = jnp.zeros((2, D, D), BF)

        @pl.when(c + step >= chips)
        def _():
            ret_in[1, step - 1] = jnp.zeros((2, D, D), BF)

        @pl.when(y + step >= RING)
        def _():
            ret_in[0, step - 1] = jnp.zeros((2, D, D), BF)

        @pl.when(y - step < 0)
        def _():
            part_in[step - 1] = jnp.zeros((2, D, D), BF)

    takes = (z_lo > 0) & (y > 0)
    gives = (c + RING < chips) & (y > 0)

    @pl.when(jnp.logical_not(gives))
    def _():
        plane_in[...] = jnp.zeros((2, D, D), BF)

    row = lax.broadcasted_iota(jnp.int32, (1, D), 1)
    q_pos = (2 * c + row // 64) * D + half * 64 + row % 64
    start = jnp.zeros((1, D), jnp.int32)
    end = jnp.int32(0)
    lengths.wait()
    for i in range(DOCS):
        end = end + len_ref[i]
        start = jnp.where(q_pos >= end, end, start)
    key_row = lax.broadcasted_iota(jnp.int32, (D, 1), 0)

    def allowed(hh, step):
        which = half if hh == 0 else 1 - half
        k_pos = (2 * (c - step) + key_row // 64) * D + which * 64 + key_row % 64
        ok = k_pos >= start
        if step == 0:
            ok = ok & (k_pos <= q_pos)
        return ok

    pl.semaphore_wait(barrier, 13)

    for by in (1, 3):
        pl.semaphore_signal(ring_met, inc=1, device_id=across(by), device_id_type=MESH)

    sides = [(4, 0), (-4, 1)]
    mine = pl.ds(pl.multiple_of(piece * 16, 16), 16)

    def first_leg(i, by, side):
        cols = pl.ds(side * 4 * D, 4 * D)
        return copy(raw.at[i, :, cols], mid.at[i, :, cols], mid_s.at[i, side], mid_r.at[i, side], along(by, x, core))

    for i in (0, 1):
        here[i].wait()
        for by, side in sides:
            first_leg(i, by, side).start()

    for dx, dk in NEAR:
        kk, xx = near(dx, dk)
        cols = pl.ds(pl.multiple_of((xx * 2 + kk) * D, D), D)
        for i in (0, 1):
            copy(raw.at[i, :, cols], kvw.at[0, 0, i, mine], near_s, near_r,
                 device(c, kk, half, xx)).start()
    cols = pl.ds(pl.multiple_of(head * D, D), D)
    for i in (0, 1):
        pltpu.make_async_copy(raw.at[i, :, cols], kvw.at[0, 0, i, mine], near_r).start()
    pl.semaphore_wait(ring_met, 2)
    pl.semaphore_signal(plane_met, inc=1, device_id=along(-1, x, core), device_id_type=MESH)
    for i, (ref, to) in enumerate(((q_in, qp), (g_in, gp))):
        for dx, dk in NEAR:
            kk, xx = near(dx, dk)
            cols = pl.ds(pl.multiple_of((xx * 2 + kk) * GROUP * D, GROUP * D), GROUP * D)
            copy(ref.at[:, cols], to.at[piece], q_s.at[i], q_r.at[i], device(c, kk, half, xx)).start()
        cols = pl.ds(pl.multiple_of(head * GROUP * D, GROUP * D), GROUP * D)
        pltpu.make_async_copy(ref.at[:, cols], to.at[piece], q_r.at[i]).start()

    landed(kvw.at[0, 0], near_r)
    def window(hh, i, step):
        return copy(kvw.at[hh, 0, i], kvw.at[hh, step, i], win_s.at[hh, i, step - 1], win_r.at[hh, i, step - 1],
                    device(c + step, core, half, x))

    def to_next_plane(i):
        return copy(kvw.at[0, 0, i], way.at[i], way_s.at[i], way_r.at[i], device(c + RING, core, half, x))

    def round_plane(i, back):
        return copy(way.at[i], kvw.at[0, RING - back, i], win_s.at[0, i, 3 - back], win_r.at[0, i, 3 - back],
                    device(c - back, core, half, x))

    def send_window(hh, i):
        if hh == 0:
            pl.when(gives)(to_next_plane(i).start)
        for step in (3, 2, 1):
            pl.when(y + step < RING if hh == 0 else c + step < chips)(window(hh, i, step).start)

    def take_window(hh, i):
        for step in (1, 2, 3):
            pl.when(c - step >= 0)(window(hh, i, step).wait_recv)

    for i in (0, 1):
        send_window(0, i)

    for i in (0, 1):
        for by, side in sides:
            first_leg(i, by, side).wait_recv()
            for j in range(4 * side, 4 * side + 4):
                copy(mid.at[i, :, pl.ds(j * D, D)], kvw.at[1, 0, i, mine], far_s.at[i], far_r.at[i],
                     along(by, j // 2, j % 2)).start()

    for i in (0, 1):
        pl.when(takes)(to_next_plane(i).wait_recv)
        for back in (1, 2, 3):
            pl.when(takes & (y - back >= 0))(round_plane(i, back).start)

    pl.semaphore_wait(plane_met, 1)
    for i in (0, 1):
        landed(kvw.at[1, 0, i], far_r.at[i])
        send_window(1, i)

    def gather(pieces, rows):
        for g in range(GROUP):
            rows[g * D:(g + 1) * D, :] = pieces[:, :, g * D:(g + 1) * D].reshape(D, D)

    landed(qp, q_r.at[0])
    gather(qp, qm)

    lanes = [slice(w * WIDE, (w + 1) * WIDE) for w in range(GROUP * D // WIDE)]
    top = [jnp.full((1, WIDE), NEG, F32) for _ in lanes]
    total = [jnp.zeros((1, WIDE), F32) for _ in lanes]
    groups = [(0, (0,)), (0, (1, 2, 3)), (1, (0,)), (1, (1, 2, 3))]

    def span(hh, steps):
        return slice((hh * 4 + steps[0]) * D, (hh * 4 + steps[-1] + 1) * D)

    def block(hh, steps, i):
        return kvw[hh, steps[0]:steps[-1] + 1, i].reshape(len(steps) * D, D)

    def scores(hh, steps):
        at = span(hh, steps)
        keys = block(hh, steps, 0)
        oks = [jnp.concatenate([allowed(hh, step)] * (WIDE // D), axis=1) for step in steps]
        ok = oks[0] if len(oks) == 1 else jnp.concatenate(oks, axis=0)
        for w, lane in enumerate(lanes):
            s = jnp.where(ok, dot(keys, qm[lane, :], NT) * (SCALE * LOG2E), NEG)
            sc[at, lane] = s
            new = jnp.maximum(top[w], jnp.max(s, axis=0, keepdims=True))
            total[w] = total[w] * jnp.exp2(top[w] - new) + jnp.sum(
                jnp.exp2(sc[at, lane] - new), axis=0, keepdims=True
            )
            top[w] = new

    def prob_grads(hh, steps):
        at = span(hh, steps)
        values = block(hh, steps, 1)
        for lane in lanes:
            pg[at, lane] = dot(values, gm[lane, :], NT)

    landed(gp, q_r.at[1])
    gather(gp, gm)
    for group in (groups[0], groups[2]):
        scores(*group)
        prob_grads(*group)
    for i in (0, 1):
        take_window(0, i)
    scores(*groups[1])
    prob_grads(*groups[1])
    take_window(1, 0)
    scores(*groups[3])

    lse = [top[w] + jnp.log(total[w]) * LOG2E for w in range(len(lanes))]
    mean = [jnp.zeros((1, WIDE), F32) for _ in lanes]

    def probs(hh, steps):
        at = span(hh, steps)
        for w, lane in enumerate(lanes):
            p = jnp.exp2(sc[at, lane] - lse[w])
            sc[at, lane] = p
            pb[at, lane] = p.astype(BF)

    def means(hh, steps):
        at = span(hh, steps)
        for w, lane in enumerate(lanes):
            mean[w] = mean[w] + jnp.sum(sc[at, lane] * pg[at, lane], axis=0, keepdims=True)

    def value_part(hh, steps):
        return dot(pb[span(hh, steps), :], gm[...], NN)

    def score_grads(hh, steps):
        at = span(hh, steps)
        for w, lane in enumerate(lanes):
            db[at, lane] = (sc[at, lane] * (pg[at, lane] - mean[w])).astype(BF)

    def key_part(hh, steps):
        return dot(db[span(hh, steps), :], qm[...], NN)

    def returned(hh, i, step, part=None):
        at, sem = ((hh, step - 1, i), (hh, i, step - 1, 0)) if part is None else (
            (hh, step - 1, i, pl.ds(part * 64, 64)), (hh, i, step - 1, part))
        return copy(ret_out.at[at], ret_in.at[at], ret_s.at[sem], ret_r.at[sem], device(c - step, core, half, x))

    halves = (0, 1)

    def in_plane(i, ahead):
        return copy(ret_out.at[0, 3 - ahead, i], part_in.at[ahead - 1, i], part_s.at[i, ahead - 1],
                    part_r.at[i, ahead - 1], device(c + ahead, core, half, x))

    def to_last_plane(i):
        return copy(part_sum.at[i], plane_in.at[i], plane_s.at[i], plane_r.at[i], device(c - RING, core, half, x))

    def send_back(hh, i, part):
        ret_out[hh, :, i] = part.astype(BF).reshape(3, D, D)
        for step in (3, 2, 1):
            if hh == 0:
                ahead = RING - step
                pl.when((z_lo > 0) & (y + ahead < RING))(in_plane(i, ahead).start)
                pl.when(y - step >= 0)(returned(hh, i, step).start)
            else:
                for chunk in halves:
                    pl.when(c - step >= 0)(returned(hh, i, step, chunk).start)

    def pass_back(i):
        for ahead in (1, 2, 3):
            pl.when(takes & (y - ahead >= 0))(in_plane(i, ahead).wait_recv)

        @pl.when(takes)
        def _():
            part = part_in[0, i].astype(F32)
            for ahead in (2, 3):
                part = part + part_in[ahead - 1, i].astype(F32)
            part_sum[i] = part.astype(BF)
            to_last_plane(i).start()

    def spread(which, i, weights, pieces, out, factor):
        blocks = kvw[:, :, i].reshape(8 * D, D).T
        full = dot(blocks, weights[...], NN)
        if factor != 1.0:
            full = full * factor
        for g in range(GROUP):
            pieces[:, :, g * D:(g + 1) * D] = full[:, g * D:(g + 1) * D].T.astype(BF).reshape(8, 16, D)
        cols = pl.ds(pl.multiple_of(head * GROUP * D, GROUP * D), GROUP * D)
        for dx, dk in NEAR:
            kk, xx = near(dx, dk)
            copy(pieces.at[kk * 4 + xx], out.at[:, cols], out_s.at[which], out_r.at[which],
                 device(c, kk, half, xx)).start()
        pltpu.make_async_copy(pieces.at[piece], out.at[:, cols], out_r.at[which]).start()

    def total_of(i):
        for step in (1, 2, 3):
            pl.when(y + step < RING)(returned(0, i, step).wait_recv)
        pl.when(gives)(to_last_plane(i).wait_recv)
        part = tot[0, i] + plane_in[i].astype(F32)
        for step in (1, 2, 3):
            part = part + ret_in[0, step - 1, i].astype(F32)
        return part.astype(BF)

    def cross(i, which):
        for step in (1, 2, 3):
            pl.when(c + step < chips)(returned(1, i, step, which).wait_recv)
        rows = slice(which * 64, which * 64 + 64)
        part = tot[1, i, rows]
        for step in (1, 2, 3):
            part = part + ret_in[1, step - 1, i, rows].astype(F32)
        far_out[i, rows] = part.astype(BF)
        for p in range(which * 4, which * 4 + 4):
            copy(far_out.at[i, pl.ds(p * 16, 16)], far_in.at[i, pl.ds(pl.multiple_of(head * 16, 16), 16)],
                 back_s.at[i], back_r.at[i], along(8, p % 4, p // 4)).start()

    probs(*groups[3])
    send_back(1, 1, value_part(*groups[3]))
    for group in groups[:3]:
        probs(*group)
        means(*group)
    take_window(1, 1)
    prob_grads(*groups[3])
    means(*groups[3])
    for chunk in halves:
        first = [(5 + n) * D + chunk * 64 for n in range(3)]
        for at in first:
            at = slice(at, at + 64)
            for w, lane in enumerate(lanes):
                db[at, lane] = (sc[at, lane] * (pg[at, lane] - mean[w])).astype(BF)
        grads = dot(jnp.concatenate([db[at:at + 64, :] for at in first], axis=0), qm[...], NN).astype(BF)
        for step in (3, 2, 1):
            ret_out[1, step - 1, 0, chunk * 64:chunk * 64 + 64] = grads[(step - 1) * 64:step * 64]
            pl.when(c - step >= 0)(returned(1, 0, step, chunk).start)
    send_back(0, 1, value_part(*groups[1]))
    score_grads(*groups[1])
    send_back(0, 0, key_part(*groups[1]))
    tot[1, 1] = value_part(*groups[2])
    score_grads(*groups[2])
    tot[1, 0] = key_part(*groups[2])
    cross(1, 0)
    cross(1, 1)
    pass_back(1)
    spread(0, 1, pb, op, o_out, 1.0)
    pass_back(0)
    @pl.when(half == 1)
    def _():
        cross(0, 0)
        cross(0, 1)

    score_grads(*groups[0])
    spread(1, 0, db, qgp, dq_out, SCALE)
    tot[0, 1] = value_part(*groups[0])
    tot[0, 0] = key_part(*groups[0])
    to = pl.ds(pl.multiple_of(head * 16, 16), 16)
    for i in (1, 0):
        own_out[i] = total_of(i)
        for dx, dk in NEAR:
            kk, xx = near(dx, dk)
            copy(own_out.at[i, pl.ds(pl.multiple_of((kk * 4 + xx) * 16, 16), 16)], own_in.at[i, to], own_s.at[i],
                 own_r.at[i], device(c, kk, half, xx)).start()
        pltpu.make_async_copy(own_out.at[i, mine], own_in.at[i, to], own_r.at[i]).start()
    @pl.when(half == 0)
    def _():
        cross(0, 0)
        cross(0, 1)

    for i, (out, factor) in ((1, (dv_out, 1.0)), (0, (dk_out, SCALE))):
        landed(own_in.at[i], own_r.at[i])
        landed(far_in.at[i], back_r.at[i])
        for j in range(8):
            both = own_in[i, j * 16:(j + 1) * 16].astype(F32) + far_in[i, j * 16:(j + 1) * 16].astype(F32)
            out[:, j * D:(j + 1) * D] = (both * factor).astype(BF)

    landed(kvw.at[0, 0, :, pl.ds(0, 112)], near_s)
    for i, ref in enumerate((qp, gp)):
        landed(ref.at[pl.ds(0, 7)], q_s.at[i])
    for i in (0, 1):
        for by, side in sides:
            first_leg(i, by, side).wait_send()
        landed(kvw.at[1, 0, i], far_s.at[i])
        pl.when(gives)(to_next_plane(i).wait_send)
        pl.when(takes)(to_last_plane(i).wait_send)
        for step in (1, 2, 3):
            pl.when(y + step < RING)(window(0, i, step).wait_send)
            pl.when(takes & (y - step >= 0))(round_plane(i, step).wait_send)
            pl.when(c + step < chips)(window(1, i, step).wait_send)
            pl.when((z_lo > 0) & (y + step < RING))(in_plane(i, step).wait_send)
            pl.when(y - step >= 0)(returned(0, i, step).wait_send)
            for chunk in halves:
                pl.when(c - step >= 0)(returned(1, i, step, chunk).wait_send)
        landed(far_out.at[i], back_s.at[i])
        landed(own_out.at[i, pl.ds(0, 112)], own_s.at[i])
    for i, ref in enumerate((op, qgp)):
        landed(ref.at[pl.ds(0, 7)], out_s.at[i])
    for i, ref in enumerate((o_out, dq_out)):
        landed(ref, out_r.at[i])


def write_out(a, b, c, d, ao, bo, co, do, sems):
    copies = [
        pltpu.make_async_copy(src, dst, sems.at[i]) for i, (src, dst) in enumerate(((a, ao), (b, bo), (c, co), (d, do)))
    ]
    for cp in copies:
        cp.start()
    for cp in copies:
        cp.wait()


def per_device(query, key, value, cotangent, doc_lengths):
    chips = lax.axis_size("dp") // 2
    rows = GROUP * D
    keys = 8 * D
    sem = pltpu.SemaphoreType.DMA
    any_ = pl.BlockSpec(memory_space=pl.ANY)
    vmem = pl.BlockSpec(memory_space=pltpu.VMEM)
    parts = pl.pallas_call(
        functools.partial(kernel, chips),
        out_shape=[jax.ShapeDtypeStruct(a.shape, BF) for a in (query, query, key, value)],
        in_specs=[any_] * 5,
        out_specs=[vmem] * 4,
        scratch_shapes=[
            pltpu.VMEM((2, 4, 2, D, D), BF),
            pltpu.VMEM((2, 16, 8 * D), BF),
            pltpu.VMEM((8, 16, rows), BF),
            pltpu.VMEM((8, 16, rows), BF),
            pltpu.VMEM((rows, D), BF),
            pltpu.VMEM((rows, D), BF),
            pltpu.VMEM((keys, rows), F32),
            pltpu.VMEM((keys, rows), F32),
            pltpu.VMEM((keys, rows), BF),
            pltpu.VMEM((keys, rows), BF),
            pltpu.VMEM((2, 3, 2, D, D), BF),
            pltpu.VMEM((2, 3, 2, D, D), BF),
            pltpu.VMEM((2, 2, D, D), F32),
            pltpu.VMEM((2, D, D), BF),
            pltpu.VMEM((2, D, D), BF),
            pltpu.VMEM((2, D, D), BF),
            pltpu.VMEM((2, D, D), BF),
            pltpu.VMEM((8, 16, rows), BF),
            pltpu.VMEM((8, 16, rows), BF),
            pltpu.VMEM((2, D, D), BF),
            pltpu.VMEM((3, 2, D, D), BF),
            pltpu.VMEM((2, D, D), BF),
            pltpu.VMEM((2, D, D), BF),
            pltpu.VMEM((2, 16, 8 * D), BF), sem((2,)),
            pltpu.SMEM((DOCS,), jnp.int32), sem, pltpu.SemaphoreType.REGULAR, pltpu.SemaphoreType.REGULAR,
            sem, sem, sem((2, 2)), sem((2, 2)), sem((2,)), sem((2,)), sem((2,)), sem((2,)),
            sem((2, 2, 3)), sem((2, 2, 3)), sem((2, 2, 3, 2)), sem((2, 2, 3, 2)),
            sem((2,)), sem((2,)), sem((2,)), sem((2,)), sem((2,)), sem((2,)),
            sem((2,)), sem((2,)), sem((2, 3)), sem((2, 3)), sem((2,)), sem((2,)),
        ],
        compiler_params=pltpu.CompilerParams(
            collective_id=0, has_side_effects=True, vmem_limit_bytes=60 << 20
        ),
        name="attention",
    )(query, key, value, cotangent, doc_lengths)
    return pl.pallas_call(
        write_out,
        out_shape=[jax.ShapeDtypeStruct(a.shape, BF) for a in parts],
        in_specs=[vmem] * 4,
        out_specs=[any_] * 4,
        scratch_shapes=[sem((4,))],
        name="write_out",
    )(*parts)


def solution(mesh):
    placed = P(("dp", "tensor"), None)
    return jax.shard_map(
        per_device,
        mesh=mesh,
        in_specs=(placed,) * 4 + (P(),),
        out_specs=(placed,) * 4,
        check_vma=False,
    )
```

```python
import functools
import math

import jax
import jax.numpy as jnp
from jax import lax
from jax.experimental import pallas as pl
from jax.experimental.pallas import tpu as pltpu
from jax.sharding import PartitionSpec as P

D = 128
GROUP = 8
DOCS = 16
SCALE = 1.0 / math.sqrt(D)
LOG2E = math.log2(math.e)
NEG = -1e30
RING = 4
MESH = pl.DeviceIdType.MESH
BF = jnp.bfloat16
F32 = jnp.float32
WIDE = 256
NT = (((1,), (1,)), ((), ()))
NN = (((1,), (0,)), ((), ()))
NEAR = [(dx, dk) for dx in (1, 3, 2, 0) for dk in (0, 1) if (dx, dk) != (0, 0)]


def dot(a, b, dims):
    return lax.dot_general(a, b, dims, preferred_element_type=F32)


def kernel(
    chips, q_in, k_in, v_in, g_in, len_in,
    o_out, dq_out, dk_out, dv_out,
    kvw, mid, qp, gp, qm, gm, sc, pg, pb, db, ret_out, ret_in, tot, far_out, far_in, own_out, own_in, op, qgp,
    way, part_in, part_sum, plane_in, raw, raw_s,
    len_ref, len_s, ring_met, plane_met, near_s, near_r, mid_s, mid_r, q_s, q_r, far_s, far_r, win_s, win_r, ret_s, ret_r, back_s, back_r,
    own_s, own_r, out_s, out_r, way_s, way_r, part_s, part_r, plane_s, plane_r,
):
    d, t = lax.axis_index("dp"), lax.axis_index("tensor")
    c, core, half, x = d // 2, d % 2, t // 4, t % 4
    z_lo, y = c // RING, c % RING
    piece = core * 4 + x
    head = x * 2 + core

    def device(cc, kk, hh, xx):
        return (cc * 2 + kk, hh * 4 + xx)

    def near(dx, dk):
        return (core + dk) % 2, (x + dx) % 4

    def along(by, xx, kk):
        z = (half * 8 + z_lo + by + 16) % 16
        return device(z % 8 * RING + y, kk, z // 8, xx)

    def copy(src, dst, ssem, rsem, to):
        return pltpu.make_async_remote_copy(
            src_ref=src, dst_ref=dst, send_sem=ssem, recv_sem=rsem, device_id=to, device_id_type=MESH
        )

    def landed(ref, sem):
        pltpu.make_async_copy(ref, ref, sem).wait()

    lengths = pltpu.make_async_copy(len_in, len_ref, len_s)
    lengths.start()
    here = [pltpu.make_async_copy((k_in, v_in)[i], raw.at[i], raw_s.at[i]) for i in (0, 1)]
    for cp in here:
        cp.start()
    barrier = pltpu.get_barrier_semaphore()

    def greet(to):
        pl.semaphore_signal(barrier, inc=1, device_id=to, device_id_type=MESH)

    def across(by):
        return device(z_lo * RING + (y + by) % RING, core, half, x)

    for by in (4, -4, 1, -1):
        greet(along(by, x, core))
    for by in (1, 3):
        greet(across(by))
    for dx, dk in NEAR:
        kk, xx = near(dx, dk)
        greet(device(c, kk, half, xx))

    for step in (1, 2, 3):
        @pl.when(c - step < 0)
        def _():
            for hh in (0, 1):
                kvw[hh, step] = jnp.zeros((2, D, D), BF)

        @pl.when(c + step >= chips)
        def _():
            ret_in[1, step - 1] = jnp.zeros((2, D, D), BF)

        @pl.when(y + step >= RING)
        def _():
            ret_in[0, step - 1] = jnp.zeros((2, D, D), BF)

        @pl.when(y - step < 0)
        def _():
            part_in[step - 1] = jnp.zeros((2, D, D), BF)

    takes = (z_lo > 0) & (y > 0)
    gives = (c + RING < chips) & (y > 0)

    @pl.when(jnp.logical_not(gives))
    def _():
        plane_in[...] = jnp.zeros((2, D, D), BF)

    row = lax.broadcasted_iota(jnp.int32, (1, D), 1)
    q_pos = (2 * c + row // 64) * D + half * 64 + row % 64
    start = jnp.zeros((1, D), jnp.int32)
    end = jnp.int32(0)
    lengths.wait()
    for i in range(DOCS):
        end = end + len_ref[i]
        start = jnp.where(q_pos >= end, end, start)
    key_row = lax.broadcasted_iota(jnp.int32, (D, 1), 0)

    def allowed(hh, step):
        which = half if hh == 0 else 1 - half
        k_pos = (2 * (c - step) + key_row // 64) * D + which * 64 + key_row % 64
        ok = k_pos >= start
        if step == 0:
            ok = ok & (k_pos <= q_pos)
        return ok

    pl.semaphore_wait(barrier, 13)

    for by in (1, 3):
        pl.semaphore_signal(ring_met, inc=1, device_id=across(by), device_id_type=MESH)

    sides = [(4, 0), (-4, 1)]
    mine = pl.ds(pl.multiple_of(piece * 16, 16), 16)

    def first_leg(i, by, side):
        cols = pl.ds(side * 4 * D, 4 * D)
        return copy(raw.at[i, :, cols], mid.at[i, :, cols], mid_s.at[i, side], mid_r.at[i, side], along(by, x, core))

    for i in (0, 1):
        here[i].wait()
        for by, side in sides:
            first_leg(i, by, side).start()

    for dx, dk in NEAR:
        kk, xx = near(dx, dk)
        cols = pl.ds(pl.multiple_of((xx * 2 + kk) * D, D), D)
        for i in (0, 1):
            copy(raw.at[i, :, cols], kvw.at[0, 0, i, mine], near_s, near_r,
                 device(c, kk, half, xx)).start()
    cols = pl.ds(pl.multiple_of(head * D, D), D)
    for i in (0, 1):
        pltpu.make_async_copy(raw.at[i, :, cols], kvw.at[0, 0, i, mine], near_r).start()
    pl.semaphore_wait(ring_met, 2)
    pl.semaphore_signal(plane_met, inc=1, device_id=along(-1, x, core), device_id_type=MESH)
    for i, (ref, to) in enumerate(((q_in, qp), (g_in, gp))):
        for dx, dk in NEAR:
            kk, xx = near(dx, dk)
            cols = pl.ds(pl.multiple_of((xx * 2 + kk) * GROUP * D, GROUP * D), GROUP * D)
            copy(ref.at[:, cols], to.at[piece], q_s.at[i], q_r.at[i], device(c, kk, half, xx)).start()
        cols = pl.ds(pl.multiple_of(head * GROUP * D, GROUP * D), GROUP * D)
        pltpu.make_async_copy(ref.at[:, cols], to.at[piece], q_r.at[i]).start()

    landed(kvw.at[0, 0], near_r)
    def window(hh, i, step):
        return copy(kvw.at[hh, 0, i], kvw.at[hh, step, i], win_s.at[hh, i, step - 1], win_r.at[hh, i, step - 1],
                    device(c + step, core, half, x))

    def to_next_plane(i):
        return copy(kvw.at[0, 0, i], way.at[i], way_s.at[i], way_r.at[i], device(c + RING, core, half, x))

    def round_plane(i, back):
        return copy(way.at[i], kvw.at[0, RING - back, i], win_s.at[0, i, 3 - back], win_r.at[0, i, 3 - back],
                    device(c - back, core, half, x))

    def send_window(hh, i):
        if hh == 0:
            pl.when(gives)(to_next_plane(i).start)
        for step in (1, 2, 3):
            pl.when(y + step < RING if hh == 0 else c + step < chips)(window(hh, i, step).start)

    def take_window(hh, i):
        for step in (1, 2, 3):
            pl.when(c - step >= 0)(window(hh, i, step).wait_recv)

    for i in (0, 1):
        send_window(0, i)

    for i in (0, 1):
        for by, side in sides:
            first_leg(i, by, side).wait_recv()
            for j in range(4 * side, 4 * side + 4):
                copy(mid.at[i, :, pl.ds(j * D, D)], kvw.at[1, 0, i, mine], far_s.at[i], far_r.at[i],
                     along(by, j // 2, j % 2)).start()

    for i in (0, 1):
        pl.when(takes)(to_next_plane(i).wait_recv)
        for back in (1, 2, 3):
            pl.when(takes & (y - back >= 0))(round_plane(i, back).start)

    pl.semaphore_wait(plane_met, 1)
    for i in (0, 1):
        landed(kvw.at[1, 0, i], far_r.at[i])
        send_window(1, i)

    def gather(pieces, rows):
        for g in range(GROUP):
            rows[g * D:(g + 1) * D, :] = pieces[:, :, g * D:(g + 1) * D].reshape(D, D)

    landed(qp, q_r.at[0])
    gather(qp, qm)

    lanes = [slice(w * WIDE, (w + 1) * WIDE) for w in range(GROUP * D // WIDE)]
    top = [jnp.full((1, WIDE), NEG, F32) for _ in lanes]
    total = [jnp.zeros((1, WIDE), F32) for _ in lanes]
    groups = [(0, (0,)), (0, (1, 2, 3)), (1, (0,)), (1, (1, 2, 3))]

    def span(hh, steps):
        return slice((hh * 4 + steps[0]) * D, (hh * 4 + steps[-1] + 1) * D)

    def block(hh, steps, i):
        return kvw[hh, steps[0]:steps[-1] + 1, i].reshape(len(steps) * D, D)

    def scores(hh, steps):
        at = span(hh, steps)
        keys = block(hh, steps, 0)
        oks = [jnp.concatenate([allowed(hh, step)] * (WIDE // D), axis=1) for step in steps]
        ok = oks[0] if len(oks) == 1 else jnp.concatenate(oks, axis=0)
        for w, lane in enumerate(lanes):
            s = jnp.where(ok, dot(keys, qm[lane, :], NT) * (SCALE * LOG2E), NEG)
            sc[at, lane] = s
            new = jnp.maximum(top[w], jnp.max(s, axis=0, keepdims=True))
            total[w] = total[w] * jnp.exp2(top[w] - new) + jnp.sum(
                jnp.exp2(sc[at, lane] - new), axis=0, keepdims=True
            )
            top[w] = new

    def prob_grads(hh, steps):
        at = span(hh, steps)
        values = block(hh, steps, 1)
        for lane in lanes:
            pg[at, lane] = dot(values, gm[lane, :], NT)

    landed(gp, q_r.at[1])
    gather(gp, gm)
    for group in (groups[0], groups[2]):
        scores(*group)
        prob_grads(*group)
    for i in (0, 1):
        take_window(0, i)
    scores(*groups[1])
    prob_grads(*groups[1])
    take_window(1, 0)
    scores(*groups[3])

    lse = [top[w] + jnp.log(total[w]) * LOG2E for w in range(len(lanes))]
    mean = [jnp.zeros((1, WIDE), F32) for _ in lanes]

    def probs(hh, steps):
        at = span(hh, steps)
        for w, lane in enumerate(lanes):
            p = jnp.exp2(sc[at, lane] - lse[w])
            sc[at, lane] = p
            pb[at, lane] = p.astype(BF)

    def means(hh, steps):
        at = span(hh, steps)
        for w, lane in enumerate(lanes):
            mean[w] = mean[w] + jnp.sum(sc[at, lane] * pg[at, lane], axis=0, keepdims=True)

    def value_part(hh, steps):
        return dot(pb[span(hh, steps), :], gm[...], NN)

    def score_grads(hh, steps):
        at = span(hh, steps)
        for w, lane in enumerate(lanes):
            db[at, lane] = (sc[at, lane] * (pg[at, lane] - mean[w])).astype(BF)

    def key_part(hh, steps):
        return dot(db[span(hh, steps), :], qm[...], NN)

    def returned(hh, i, step, part=None):
        at, sem = ((hh, step - 1, i), (hh, i, step - 1, 0)) if part is None else (
            (hh, step - 1, i, pl.ds(part * 64, 64)), (hh, i, step - 1, part))
        return copy(ret_out.at[at], ret_in.at[at], ret_s.at[sem], ret_r.at[sem], device(c - step, core, half, x))

    halves = (0, 1)

    def in_plane(i, ahead):
        return copy(ret_out.at[0, 3 - ahead, i], part_in.at[ahead - 1, i], part_s.at[i, ahead - 1],
                    part_r.at[i, ahead - 1], device(c + ahead, core, half, x))

    def to_last_plane(i):
        return copy(part_sum.at[i], plane_in.at[i], plane_s.at[i], plane_r.at[i], device(c - RING, core, half, x))

    def send_back(hh, i, part):
        ret_out[hh, :, i] = part.astype(BF).reshape(3, D, D)
        for step in (1, 2, 3):
            if hh == 0:
                ahead = RING - step
                pl.when((z_lo > 0) & (y + ahead < RING))(in_plane(i, ahead).start)
                pl.when(y - step >= 0)(returned(hh, i, step).start)
            else:
                for chunk in halves:
                    pl.when(c - step >= 0)(returned(hh, i, step, chunk).start)

    def pass_back(i):
        for ahead in (1, 2, 3):
            pl.when(takes & (y - ahead >= 0))(in_plane(i, ahead).wait_recv)

        @pl.when(takes)
        def _():
            part = part_in[0, i].astype(F32)
            for ahead in (2, 3):
                part = part + part_in[ahead - 1, i].astype(F32)
            part_sum[i] = part.astype(BF)
            to_last_plane(i).start()

    def spread(which, i, weights, pieces, out, factor):
        blocks = kvw[:, :, i].reshape(8 * D, D).T
        full = dot(blocks, weights[...], NN)
        if factor != 1.0:
            full = full * factor
        for g in range(GROUP):
            pieces[:, :, g * D:(g + 1) * D] = full[:, g * D:(g + 1) * D].T.astype(BF).reshape(8, 16, D)
        cols = pl.ds(pl.multiple_of(head * GROUP * D, GROUP * D), GROUP * D)
        for dx, dk in NEAR:
            kk, xx = near(dx, dk)
            copy(pieces.at[kk * 4 + xx], out.at[:, cols], out_s.at[which], out_r.at[which],
                 device(c, kk, half, xx)).start()
        pltpu.make_async_copy(pieces.at[piece], out.at[:, cols], out_r.at[which]).start()

    def total_of(i):
        for step in (1, 2, 3):
            pl.when(y + step < RING)(returned(0, i, step).wait_recv)
        pl.when(gives)(to_last_plane(i).wait_recv)
        part = tot[0, i] + plane_in[i].astype(F32)
        for step in (1, 2, 3):
            part = part + ret_in[0, step - 1, i].astype(F32)
        return part.astype(BF)

    def cross(i, which):
        for step in (1, 2, 3):
            pl.when(c + step < chips)(returned(1, i, step, which).wait_recv)
        rows = slice(which * 64, which * 64 + 64)
        part = tot[1, i, rows]
        for step in (1, 2, 3):
            part = part + ret_in[1, step - 1, i, rows].astype(F32)
        far_out[i, rows] = part.astype(BF)
        for p in range(which * 4, which * 4 + 4):
            copy(far_out.at[i, pl.ds(p * 16, 16)], far_in.at[i, pl.ds(pl.multiple_of(head * 16, 16), 16)],
                 back_s.at[i], back_r.at[i], along(8, p % 4, p // 4)).start()

    probs(*groups[3])
    send_back(1, 1, value_part(*groups[3]))
    for group in groups[:3]:
        probs(*group)
        means(*group)
    take_window(1, 1)
    prob_grads(*groups[3])
    means(*groups[3])
    for chunk in halves:
        first = [(5 + n) * D + chunk * 64 for n in range(3)]
        for at in first:
            at = slice(at, at + 64)
            for w, lane in enumerate(lanes):
                db[at, lane] = (sc[at, lane] * (pg[at, lane] - mean[w])).astype(BF)
        grads = dot(jnp.concatenate([db[at:at + 64, :] for at in first], axis=0), qm[...], NN).astype(BF)
        for step in (1, 2, 3):
            ret_out[1, step - 1, 0, chunk * 64:chunk * 64 + 64] = grads[(step - 1) * 64:step * 64]
            pl.when(c - step >= 0)(returned(1, 0, step, chunk).start)
    send_back(0, 1, value_part(*groups[1]))
    score_grads(*groups[1])
    send_back(0, 0, key_part(*groups[1]))
    tot[1, 1] = value_part(*groups[2])
    score_grads(*groups[2])
    tot[1, 0] = key_part(*groups[2])
    cross(1, 0)
    cross(1, 1)
    pl.when(half == 0)(lambda: pass_back(1))
    spread(0, 1, pb, op, o_out, 1.0)
    pl.when(half == 0)(lambda: pass_back(0))

    @pl.when(half == 1)
    def _():
        cross(0, 0)
        cross(0, 1)
        pass_back(1)
        pass_back(0)

    score_grads(*groups[0])
    spread(1, 0, db, qgp, dq_out, SCALE)
    tot[0, 1] = value_part(*groups[0])
    tot[0, 0] = key_part(*groups[0])
    to = pl.ds(pl.multiple_of(head * 16, 16), 16)
    for i in (1, 0):
        own_out[i] = total_of(i)
        for dx, dk in NEAR:
            kk, xx = near(dx, dk)
            copy(own_out.at[i, pl.ds(pl.multiple_of((kk * 4 + xx) * 16, 16), 16)], own_in.at[i, to], own_s.at[i],
                 own_r.at[i], device(c, kk, half, xx)).start()
        pltpu.make_async_copy(own_out.at[i, mine], own_in.at[i, to], own_r.at[i]).start()
    @pl.when(half == 0)
    def _():
        cross(0, 0)
        cross(0, 1)

    for i, (out, factor) in ((1, (dv_out, 1.0)), (0, (dk_out, SCALE))):
        landed(own_in.at[i], own_r.at[i])
        landed(far_in.at[i], back_r.at[i])
        for j in range(8):
            both = own_in[i, j * 16:(j + 1) * 16].astype(F32) + far_in[i, j * 16:(j + 1) * 16].astype(F32)
            out[:, j * D:(j + 1) * D] = (both * factor).astype(BF)

    landed(kvw.at[0, 0, :, pl.ds(0, 112)], near_s)
    for i, ref in enumerate((qp, gp)):
        landed(ref.at[pl.ds(0, 7)], q_s.at[i])
    for i in (0, 1):
        for by, side in sides:
            first_leg(i, by, side).wait_send()
        landed(kvw.at[1, 0, i], far_s.at[i])
        pl.when(gives)(to_next_plane(i).wait_send)
        pl.when(takes)(to_last_plane(i).wait_send)
        for step in (1, 2, 3):
            pl.when(y + step < RING)(window(0, i, step).wait_send)
            pl.when(takes & (y - step >= 0))(round_plane(i, step).wait_send)
            pl.when(c + step < chips)(window(1, i, step).wait_send)
            pl.when((z_lo > 0) & (y + step < RING))(in_plane(i, step).wait_send)
            pl.when(y - step >= 0)(returned(0, i, step).wait_send)
            for chunk in halves:
                pl.when(c - step >= 0)(returned(1, i, step, chunk).wait_send)
        landed(far_out.at[i], back_s.at[i])
        landed(own_out.at[i, pl.ds(0, 112)], own_s.at[i])
    for i, ref in enumerate((op, qgp)):
        landed(ref.at[pl.ds(0, 7)], out_s.at[i])
    for i, ref in enumerate((o_out, dq_out)):
        landed(ref, out_r.at[i])


def write_out(a, b, c, d, ao, bo, co, do, sems):
    copies = [
        pltpu.make_async_copy(src, dst, sems.at[i]) for i, (src, dst) in enumerate(((a, ao), (b, bo), (c, co), (d, do)))
    ]
    for cp in copies:
        cp.start()
    for cp in copies:
        cp.wait()


def per_device(query, key, value, cotangent, doc_lengths):
    chips = lax.axis_size("dp") // 2
    rows = GROUP * D
    keys = 8 * D
    sem = pltpu.SemaphoreType.DMA
    any_ = pl.BlockSpec(memory_space=pl.ANY)
    vmem = pl.BlockSpec(memory_space=pltpu.VMEM)
    parts = pl.pallas_call(
        functools.partial(kernel, chips),
        out_shape=[jax.ShapeDtypeStruct(a.shape, BF) for a in (query, query, key, value)],
        in_specs=[any_] * 5,
        out_specs=[vmem] * 4,
        scratch_shapes=[
            pltpu.VMEM((2, 4, 2, D, D), BF),
            pltpu.VMEM((2, 16, 8 * D), BF),
            pltpu.VMEM((8, 16, rows), BF),
            pltpu.VMEM((8, 16, rows), BF),
            pltpu.VMEM((rows, D), BF),
            pltpu.VMEM((rows, D), BF),
            pltpu.VMEM((keys, rows), F32),
            pltpu.VMEM((keys, rows), F32),
            pltpu.VMEM((keys, rows), BF),
            pltpu.VMEM((keys, rows), BF),
            pltpu.VMEM((2, 3, 2, D, D), BF),
            pltpu.VMEM((2, 3, 2, D, D), BF),
            pltpu.VMEM((2, 2, D, D), F32),
            pltpu.VMEM((2, D, D), BF),
            pltpu.VMEM((2, D, D), BF),
            pltpu.VMEM((2, D, D), BF),
            pltpu.VMEM((2, D, D), BF),
            pltpu.VMEM((8, 16, rows), BF),
            pltpu.VMEM((8, 16, rows), BF),
            pltpu.VMEM((2, D, D), BF),
            pltpu.VMEM((3, 2, D, D), BF),
            pltpu.VMEM((2, D, D), BF),
            pltpu.VMEM((2, D, D), BF),
            pltpu.VMEM((2, 16, 8 * D), BF), sem((2,)),
            pltpu.SMEM((DOCS,), jnp.int32), sem, pltpu.SemaphoreType.REGULAR, pltpu.SemaphoreType.REGULAR,
            sem, sem, sem((2, 2)), sem((2, 2)), sem((2,)), sem((2,)), sem((2,)), sem((2,)),
            sem((2, 2, 3)), sem((2, 2, 3)), sem((2, 2, 3, 2)), sem((2, 2, 3, 2)),
            sem((2,)), sem((2,)), sem((2,)), sem((2,)), sem((2,)), sem((2,)),
            sem((2,)), sem((2,)), sem((2, 3)), sem((2, 3)), sem((2,)), sem((2,)),
        ],
        compiler_params=pltpu.CompilerParams(
            collective_id=0, has_side_effects=True, vmem_limit_bytes=60 << 20
        ),
        name="attention",
    )(query, key, value, cotangent, doc_lengths)
    return pl.pallas_call(
        write_out,
        out_shape=[jax.ShapeDtypeStruct(a.shape, BF) for a in parts],
        in_specs=[vmem] * 4,
        out_specs=[any_] * 4,
        scratch_shapes=[sem((4,))],
        name="write_out",
    )(*parts)


def solution(mesh):
    placed = P(("dp", "tensor"), None)
    return jax.shard_map(
        per_device,
        mesh=mesh,
        in_specs=(placed,) * 4 + (P(),),
        out_specs=(placed,) * 4,
        check_vma=False,
    )
```

```python
import functools
import math

import jax
import jax.numpy as jnp
from jax import lax
from jax.experimental import pallas as pl
from jax.experimental.pallas import tpu as pltpu
from jax.sharding import PartitionSpec as P

D = 128
GROUP = 8
DOCS = 16
SCALE = 1.0 / math.sqrt(D)
LOG2E = math.log2(math.e)
NEG = -1e30
RING = 4
MESH = pl.DeviceIdType.MESH
BF = jnp.bfloat16
F32 = jnp.float32
WIDE = 256
NT = (((1,), (1,)), ((), ()))
NN = (((1,), (0,)), ((), ()))
NEAR = [(dx, dk) for dx in (1, 3, 2, 0) for dk in (0, 1) if (dx, dk) != (0, 0)]


def dot(a, b, dims):
    return lax.dot_general(a, b, dims, preferred_element_type=F32)


def kernel(
    chips, q_in, k_in, v_in, g_in, len_in,
    o_out, dq_out, dk_out, dv_out,
    kvw, mid, qp, gp, qm, gm, sc, pg, pb, db, ret_out, ret_in, tot, far_out, far_in, own_out, own_in, op, qgp,
    way, part_in, part_sum, plane_in, raw, raw_s,
    len_ref, len_s, ring_met, plane_met, near_s, near_r, mid_s, mid_r, q_s, q_r, far_s, far_r, win_s, win_r, ret_s, ret_r, back_s, back_r,
    own_s, own_r, out_s, out_r, way_s, way_r, part_s, part_r, plane_s, plane_r,
):
    d, t = lax.axis_index("dp"), lax.axis_index("tensor")
    c, core, half, x = d // 2, d % 2, t // 4, t % 4
    z_lo, y = c // RING, c % RING
    piece = core * 4 + x
    head = x * 2 + core

    def device(cc, kk, hh, xx):
        return (cc * 2 + kk, hh * 4 + xx)

    def near(dx, dk):
        return (core + dk) % 2, (x + dx) % 4

    def along(by, xx, kk):
        z = (half * 8 + z_lo + by + 16) % 16
        return device(z % 8 * RING + y, kk, z // 8, xx)

    def copy(src, dst, ssem, rsem, to):
        return pltpu.make_async_remote_copy(
            src_ref=src, dst_ref=dst, send_sem=ssem, recv_sem=rsem, device_id=to, device_id_type=MESH
        )

    def landed(ref, sem):
        pltpu.make_async_copy(ref, ref, sem).wait()

    lengths = pltpu.make_async_copy(len_in, len_ref, len_s)
    lengths.start()
    here = [pltpu.make_async_copy((k_in, v_in)[i], raw.at[i], raw_s.at[i]) for i in (0, 1)]
    for cp in here:
        cp.start()
    barrier = pltpu.get_barrier_semaphore()

    def greet(to):
        pl.semaphore_signal(barrier, inc=1, device_id=to, device_id_type=MESH)

    def across(by):
        return device(z_lo * RING + (y + by) % RING, core, half, x)

    for by in (4, -4, 1, -1):
        greet(along(by, x, core))
    for by in (1, 3):
        greet(across(by))
    for dx, dk in NEAR:
        kk, xx = near(dx, dk)
        greet(device(c, kk, half, xx))

    for step in (1, 2, 3):
        @pl.when(c - step < 0)
        def _():
            for hh in (0, 1):
                kvw[hh, step] = jnp.zeros((2, D, D), BF)

        @pl.when(c + step >= chips)
        def _():
            ret_in[1, step - 1] = jnp.zeros((2, D, D), BF)

        @pl.when(y + step >= RING)
        def _():
            ret_in[0, step - 1] = jnp.zeros((2, D, D), BF)

        @pl.when(y - step < 0)
        def _():
            part_in[step - 1] = jnp.zeros((2, D, D), BF)

    takes = (z_lo > 0) & (y > 0)
    gives = (c + RING < chips) & (y > 0)

    @pl.when(jnp.logical_not(gives))
    def _():
        plane_in[...] = jnp.zeros((2, D, D), BF)

    row = lax.broadcasted_iota(jnp.int32, (1, D), 1)
    q_pos = (2 * c + row // 64) * D + half * 64 + row % 64
    start = jnp.zeros((1, D), jnp.int32)
    end = jnp.int32(0)
    lengths.wait()
    for i in range(DOCS):
        end = end + len_ref[i]
        start = jnp.where(q_pos >= end, end, start)
    key_row = lax.broadcasted_iota(jnp.int32, (D, 1), 0)

    def allowed(hh, step):
        which = half if hh == 0 else 1 - half
        k_pos = (2 * (c - step) + key_row // 64) * D + which * 64 + key_row % 64
        ok = k_pos >= start
        if step == 0:
            ok = ok & (k_pos <= q_pos)
        return ok

    pl.semaphore_wait(barrier, 13)

    for by in (1, 3):
        pl.semaphore_signal(ring_met, inc=1, device_id=across(by), device_id_type=MESH)

    sides = [(4, 0), (-4, 1)]
    mine = pl.ds(pl.multiple_of(piece * 16, 16), 16)

    def first_leg(i, by, side):
        cols = pl.ds(side * 4 * D, 4 * D)
        return copy(raw.at[i, :, cols], mid.at[i, :, cols], mid_s.at[i, side], mid_r.at[i, side], along(by, x, core))

    for i in (0, 1):
        here[i].wait()
        for by, side in sides:
            first_leg(i, by, side).start()

    for dx, dk in NEAR:
        kk, xx = near(dx, dk)
        cols = pl.ds(pl.multiple_of((xx * 2 + kk) * D, D), D)
        for i in (0, 1):
            copy(raw.at[i, :, cols], kvw.at[0, 0, i, mine], near_s, near_r,
                 device(c, kk, half, xx)).start()
    cols = pl.ds(pl.multiple_of(head * D, D), D)
    for i in (0, 1):
        pltpu.make_async_copy(raw.at[i, :, cols], kvw.at[0, 0, i, mine], near_r).start()
    pl.semaphore_wait(ring_met, 2)
    pl.semaphore_signal(plane_met, inc=1, device_id=along(-1, x, core), device_id_type=MESH)
    for i, (ref, to) in enumerate(((q_in, qp), (g_in, gp))):
        for dx, dk in NEAR:
            kk, xx = near(dx, dk)
            cols = pl.ds(pl.multiple_of((xx * 2 + kk) * GROUP * D, GROUP * D), GROUP * D)
            copy(ref.at[:, cols], to.at[piece], q_s.at[i], q_r.at[i], device(c, kk, half, xx)).start()
        cols = pl.ds(pl.multiple_of(head * GROUP * D, GROUP * D), GROUP * D)
        pltpu.make_async_copy(ref.at[:, cols], to.at[piece], q_r.at[i]).start()

    for i in (0, 1):
        for by, side in sides:
            first_leg(i, by, side).wait_recv()
        for by, side in sides:
            for j in range(4 * side, 4 * side + 4):
                copy(mid.at[i, :, pl.ds(j * D, D)], kvw.at[1, 0, i, mine], far_s.at[i], far_r.at[i],
                     along(by, j // 2, j % 2)).start()

    landed(kvw.at[0, 0], near_r)
    def window(hh, i, step):
        return copy(kvw.at[hh, 0, i], kvw.at[hh, step, i], win_s.at[hh, i, step - 1], win_r.at[hh, i, step - 1],
                    device(c + step, core, half, x))

    def to_next_plane(i):
        return copy(kvw.at[0, 0, i], way.at[i], way_s.at[i], way_r.at[i], device(c + RING, core, half, x))

    def round_plane(i, back):
        return copy(way.at[i], kvw.at[0, RING - back, i], win_s.at[0, i, 3 - back], win_r.at[0, i, 3 - back],
                    device(c - back, core, half, x))

    def send_window(hh, i):
        if hh == 0:
            pl.when(gives)(to_next_plane(i).start)
        for step in (1, 2, 3):
            pl.when(y + step < RING if hh == 0 else c + step < chips)(window(hh, i, step).start)

    def take_window(hh, i):
        for step in (1, 2, 3):
            pl.when(c - step >= 0)(window(hh, i, step).wait_recv)

    for i in (0, 1):
        send_window(0, i)

    for i in (0, 1):
        pl.when(takes)(to_next_plane(i).wait_recv)
        for back in (1, 2, 3):
            pl.when(takes & (y - back >= 0))(round_plane(i, back).start)

    pl.semaphore_wait(plane_met, 1)
    for i in (0, 1):
        landed(kvw.at[1, 0, i], far_r.at[i])
        send_window(1, i)

    def gather(pieces, rows):
        for g in range(GROUP):
            rows[g * D:(g + 1) * D, :] = pieces[:, :, g * D:(g + 1) * D].reshape(D, D)

    landed(qp, q_r.at[0])
    gather(qp, qm)

    lanes = [slice(w * WIDE, (w + 1) * WIDE) for w in range(GROUP * D // WIDE)]
    top = [jnp.full((1, WIDE), NEG, F32) for _ in lanes]
    total = [jnp.zeros((1, WIDE), F32) for _ in lanes]
    groups = [(0, (0,)), (0, (1, 2, 3)), (1, (0,)), (1, (1, 2, 3))]

    def span(hh, steps):
        return slice((hh * 4 + steps[0]) * D, (hh * 4 + steps[-1] + 1) * D)

    def block(hh, steps, i):
        return kvw[hh, steps[0]:steps[-1] + 1, i].reshape(len(steps) * D, D)

    def scores(hh, steps):
        at = span(hh, steps)
        keys = block(hh, steps, 0)
        oks = [jnp.concatenate([allowed(hh, step)] * (WIDE // D), axis=1) for step in steps]
        ok = oks[0] if len(oks) == 1 else jnp.concatenate(oks, axis=0)
        for w, lane in enumerate(lanes):
            s = jnp.where(ok, dot(keys, qm[lane, :], NT) * (SCALE * LOG2E), NEG)
            sc[at, lane] = s
            new = jnp.maximum(top[w], jnp.max(s, axis=0, keepdims=True))
            total[w] = total[w] * jnp.exp2(top[w] - new) + jnp.sum(
                jnp.exp2(sc[at, lane] - new), axis=0, keepdims=True
            )
            top[w] = new

    def prob_grads(hh, steps):
        at = span(hh, steps)
        values = block(hh, steps, 1)
        for lane in lanes:
            pg[at, lane] = dot(values, gm[lane, :], NT)

    landed(gp, q_r.at[1])
    gather(gp, gm)
    for group in (groups[0], groups[2]):
        scores(*group)
        prob_grads(*group)
    for i in (0, 1):
        take_window(0, i)
    scores(*groups[1])
    prob_grads(*groups[1])
    take_window(1, 0)
    scores(*groups[3])

    lse = [top[w] + jnp.log(total[w]) * LOG2E for w in range(len(lanes))]
    mean = [jnp.zeros((1, WIDE), F32) for _ in lanes]

    def probs(hh, steps):
        at = span(hh, steps)
        for w, lane in enumerate(lanes):
            p = jnp.exp2(sc[at, lane] - lse[w])
            sc[at, lane] = p
            pb[at, lane] = p.astype(BF)

    def means(hh, steps):
        at = span(hh, steps)
        for w, lane in enumerate(lanes):
            mean[w] = mean[w] + jnp.sum(sc[at, lane] * pg[at, lane], axis=0, keepdims=True)

    def value_part(hh, steps):
        return dot(pb[span(hh, steps), :], gm[...], NN)

    def score_grads(hh, steps):
        at = span(hh, steps)
        for w, lane in enumerate(lanes):
            db[at, lane] = (sc[at, lane] * (pg[at, lane] - mean[w])).astype(BF)

    def key_part(hh, steps):
        return dot(db[span(hh, steps), :], qm[...], NN)

    def returned(hh, i, step, part=None):
        at, sem = ((hh, step - 1, i), (hh, i, step - 1, 0)) if part is None else (
            (hh, step - 1, i, pl.ds(part * 64, 64)), (hh, i, step - 1, part))
        return copy(ret_out.at[at], ret_in.at[at], ret_s.at[sem], ret_r.at[sem], device(c - step, core, half, x))

    halves = (0, 1)

    def in_plane(i, ahead):
        return copy(ret_out.at[0, 3 - ahead, i], part_in.at[ahead - 1, i], part_s.at[i, ahead - 1],
                    part_r.at[i, ahead - 1], device(c + ahead, core, half, x))

    def to_last_plane(i):
        return copy(part_sum.at[i], plane_in.at[i], plane_s.at[i], plane_r.at[i], device(c - RING, core, half, x))

    def send_back(hh, i, part):
        ret_out[hh, :, i] = part.astype(BF).reshape(3, D, D)
        for step in (1, 2, 3):
            if hh == 0:
                ahead = RING - step
                pl.when((z_lo > 0) & (y + ahead < RING))(in_plane(i, ahead).start)
                pl.when(y - step >= 0)(returned(hh, i, step).start)
            else:
                for chunk in halves:
                    pl.when(c - step >= 0)(returned(hh, i, step, chunk).start)

    def pass_back(i):
        for ahead in (1, 2, 3):
            pl.when(takes & (y - ahead >= 0))(in_plane(i, ahead).wait_recv)

        @pl.when(takes)
        def _():
            part = part_in[0, i].astype(F32)
            for ahead in (2, 3):
                part = part + part_in[ahead - 1, i].astype(F32)
            part_sum[i] = part.astype(BF)
            to_last_plane(i).start()

    def spread(which, i, weights, pieces, out, factor):
        blocks = kvw[:, :, i].reshape(8 * D, D).T
        full = dot(blocks, weights[...], NN)
        if factor != 1.0:
            full = full * factor
        for g in range(GROUP):
            pieces[:, :, g * D:(g + 1) * D] = full[:, g * D:(g + 1) * D].T.astype(BF).reshape(8, 16, D)
        cols = pl.ds(pl.multiple_of(head * GROUP * D, GROUP * D), GROUP * D)
        for dx, dk in NEAR:
            kk, xx = near(dx, dk)
            copy(pieces.at[kk * 4 + xx], out.at[:, cols], out_s.at[which], out_r.at[which],
                 device(c, kk, half, xx)).start()
        pltpu.make_async_copy(pieces.at[piece], out.at[:, cols], out_r.at[which]).start()

    def total_of(i):
        for step in (1, 2, 3):
            pl.when(y + step < RING)(returned(0, i, step).wait_recv)
        pl.when(gives)(to_last_plane(i).wait_recv)
        part = tot[0, i] + plane_in[i].astype(F32)
        for step in (1, 2, 3):
            part = part + ret_in[0, step - 1, i].astype(F32)
        return part.astype(BF)

    def cross(i, which):
        for step in (1, 2, 3):
            pl.when(c + step < chips)(returned(1, i, step, which).wait_recv)
        rows = slice(which * 64, which * 64 + 64)
        part = tot[1, i, rows]
        for step in (1, 2, 3):
            part = part + ret_in[1, step - 1, i, rows].astype(F32)
        far_out[i, rows] = part.astype(BF)
        for p in range(which * 4, which * 4 + 4):
            copy(far_out.at[i, pl.ds(p * 16, 16)], far_in.at[i, pl.ds(pl.multiple_of(head * 16, 16), 16)],
                 back_s.at[i], back_r.at[i], along(8, p % 4, p // 4)).start()

    probs(*groups[3])
    send_back(1, 1, value_part(*groups[3]))
    for group in groups[:3]:
        probs(*group)
        means(*group)
    take_window(1, 1)
    prob_grads(*groups[3])
    means(*groups[3])
    for chunk in halves:
        first = [(5 + n) * D + chunk * 64 for n in range(3)]
        for at in first:
            at = slice(at, at + 64)
            for w, lane in enumerate(lanes):
                db[at, lane] = (sc[at, lane] * (pg[at, lane] - mean[w])).astype(BF)
        grads = dot(jnp.concatenate([db[at:at + 64, :] for at in first], axis=0), qm[...], NN).astype(BF)
        for step in (1, 2, 3):
            ret_out[1, step - 1, 0, chunk * 64:chunk * 64 + 64] = grads[(step - 1) * 64:step * 64]
            pl.when(c - step >= 0)(returned(1, 0, step, chunk).start)
    send_back(0, 1, value_part(*groups[1]))
    score_grads(*groups[1])
    send_back(0, 0, key_part(*groups[1]))
    tot[1, 1] = value_part(*groups[2])
    score_grads(*groups[2])
    tot[1, 0] = key_part(*groups[2])
    cross(1, 0)
    cross(1, 1)
    pl.when(half == 0)(lambda: pass_back(1))
    spread(0, 1, pb, op, o_out, 1.0)
    pl.when(half == 0)(lambda: pass_back(0))

    @pl.when(half == 1)
    def _():
        cross(0, 0)
        cross(0, 1)
        pass_back(1)
        pass_back(0)

    score_grads(*groups[0])
    spread(1, 0, db, qgp, dq_out, SCALE)
    tot[0, 1] = value_part(*groups[0])
    tot[0, 0] = key_part(*groups[0])
    to = pl.ds(pl.multiple_of(head * 16, 16), 16)
    for i in (1, 0):
        own_out[i] = total_of(i)
        for dx, dk in NEAR:
            kk, xx = near(dx, dk)
            copy(own_out.at[i, pl.ds(pl.multiple_of((kk * 4 + xx) * 16, 16), 16)], own_in.at[i, to], own_s.at[i],
                 own_r.at[i], device(c, kk, half, xx)).start()
        pltpu.make_async_copy(own_out.at[i, mine], own_in.at[i, to], own_r.at[i]).start()
    @pl.when(half == 0)
    def _():
        cross(0, 0)
        cross(0, 1)

    for i, (out, factor) in ((1, (dv_out, 1.0)), (0, (dk_out, SCALE))):
        landed(own_in.at[i], own_r.at[i])
        landed(far_in.at[i], back_r.at[i])
        for j in range(8):
            both = own_in[i, j * 16:(j + 1) * 16].astype(F32) + far_in[i, j * 16:(j + 1) * 16].astype(F32)
            out[:, j * D:(j + 1) * D] = (both * factor).astype(BF)

    landed(kvw.at[0, 0, :, pl.ds(0, 112)], near_s)
    for i, ref in enumerate((qp, gp)):
        landed(ref.at[pl.ds(0, 7)], q_s.at[i])
    for i in (0, 1):
        for by, side in sides:
            first_leg(i, by, side).wait_send()
        landed(kvw.at[1, 0, i], far_s.at[i])
        pl.when(gives)(to_next_plane(i).wait_send)
        pl.when(takes)(to_last_plane(i).wait_send)
        for step in (1, 2, 3):
            pl.when(y + step < RING)(window(0, i, step).wait_send)
            pl.when(takes & (y - step >= 0))(round_plane(i, step).wait_send)
            pl.when(c + step < chips)(window(1, i, step).wait_send)
            pl.when((z_lo > 0) & (y + step < RING))(in_plane(i, step).wait_send)
            pl.when(y - step >= 0)(returned(0, i, step).wait_send)
            for chunk in halves:
                pl.when(c - step >= 0)(returned(1, i, step, chunk).wait_send)
        landed(far_out.at[i], back_s.at[i])
        landed(own_out.at[i, pl.ds(0, 112)], own_s.at[i])
    for i, ref in enumerate((op, qgp)):
        landed(ref.at[pl.ds(0, 7)], out_s.at[i])
    for i, ref in enumerate((o_out, dq_out)):
        landed(ref, out_r.at[i])


def write_out(a, b, c, d, ao, bo, co, do, sems):
    copies = [
        pltpu.make_async_copy(src, dst, sems.at[i]) for i, (src, dst) in enumerate(((a, ao), (b, bo), (c, co), (d, do)))
    ]
    for cp in copies:
        cp.start()
    for cp in copies:
        cp.wait()


def per_device(query, key, value, cotangent, doc_lengths):
    chips = lax.axis_size("dp") // 2
    rows = GROUP * D
    keys = 8 * D
    sem = pltpu.SemaphoreType.DMA
    any_ = pl.BlockSpec(memory_space=pl.ANY)
    vmem = pl.BlockSpec(memory_space=pltpu.VMEM)
    parts = pl.pallas_call(
        functools.partial(kernel, chips),
        out_shape=[jax.ShapeDtypeStruct(a.shape, BF) for a in (query, query, key, value)],
        in_specs=[any_] * 5,
        out_specs=[vmem] * 4,
        scratch_shapes=[
            pltpu.VMEM((2, 4, 2, D, D), BF),
            pltpu.VMEM((2, 16, 8 * D), BF),
            pltpu.VMEM((8, 16, rows), BF),
            pltpu.VMEM((8, 16, rows), BF),
            pltpu.VMEM((rows, D), BF),
            pltpu.VMEM((rows, D), BF),
            pltpu.VMEM((keys, rows), F32),
            pltpu.VMEM((keys, rows), F32),
            pltpu.VMEM((keys, rows), BF),
            pltpu.VMEM((keys, rows), BF),
            pltpu.VMEM((2, 3, 2, D, D), BF),
            pltpu.VMEM((2, 3, 2, D, D), BF),
            pltpu.VMEM((2, 2, D, D), F32),
            pltpu.VMEM((2, D, D), BF),
            pltpu.VMEM((2, D, D), BF),
            pltpu.VMEM((2, D, D), BF),
            pltpu.VMEM((2, D, D), BF),
            pltpu.VMEM((8, 16, rows), BF),
            pltpu.VMEM((8, 16, rows), BF),
            pltpu.VMEM((2, D, D), BF),
            pltpu.VMEM((3, 2, D, D), BF),
            pltpu.VMEM((2, D, D), BF),
            pltpu.VMEM((2, D, D), BF),
            pltpu.VMEM((2, 16, 8 * D), BF), sem((2,)),
            pltpu.SMEM((DOCS,), jnp.int32), sem, pltpu.SemaphoreType.REGULAR, pltpu.SemaphoreType.REGULAR,
            sem, sem, sem((2, 2)), sem((2, 2)), sem((2,)), sem((2,)), sem((2,)), sem((2,)),
            sem((2, 2, 3)), sem((2, 2, 3)), sem((2, 2, 3, 2)), sem((2, 2, 3, 2)),
            sem((2,)), sem((2,)), sem((2,)), sem((2,)), sem((2,)), sem((2,)),
            sem((2,)), sem((2,)), sem((2, 3)), sem((2, 3)), sem((2,)), sem((2,)),
        ],
        compiler_params=pltpu.CompilerParams(
            collective_id=0, has_side_effects=True, vmem_limit_bytes=60 << 20
        ),
        name="attention",
    )(query, key, value, cotangent, doc_lengths)
    return pl.pallas_call(
        write_out,
        out_shape=[jax.ShapeDtypeStruct(a.shape, BF) for a in parts],
        in_specs=[vmem] * 4,
        out_specs=[any_] * 4,
        scratch_shapes=[sem((4,))],
        name="write_out",
    )(*parts)


def solution(mesh):
    placed = P(("dp", "tensor"), None)
    return jax.shard_map(
        per_device,
        mesh=mesh,
        in_specs=(placed,) * 4 + (P(),),
        out_specs=(placed,) * 4,
        check_vma=False,
    )
```
